32 devices in a mesh: dp: 8 (over z, y), mp: 4 (over x, core).
Axes of the slice: x: 2, y: 2, z: 4, core: 2. Of those that a mesh axis runs over, the one named last changes fastest.
Arguments:
- roll_x: bfloat16 [256, 16, 8192], P('dp', None, 'mp'), may hold values from -6 to 6
- lengths: int32 [256], P('dp'), may hold values from 1 to 16, as said below
- dest: int32 [256], P('dp'), may hold values from 0 to 7, as said below
- offsets: int32 [256], P('dp'), may hold values from 0 to 496, as said below
- queries: bfloat16 [4096, 4096], P('dp', 'mp'), may hold values from -240 to 240
- out_grad: bfloat16 [4096, 4096], P('dp', 'mp'), may hold values from -6 to 6
- w_key: bfloat16 [8192, 512], P('mp'), may hold values from -0.0625 to 0.0625
- w_value: bfloat16 [8192, 512], P('mp'), may hold values from -0.0625 to 0.0625
Outputs:
- attn_out: bfloat16 [4096, 4096], P('dp', 'mp')
- grad_x: bfloat16 [4096, 8192], P('dp', 'mp')
- grad_wk: float32 [8192, 512], P(('mp', 'dp'))
- grad_wv: float32 [8192, 512], P(('mp', 'dp'))
The draws below stay inside these ranges and needn't reach their ends.
Inputs may be any that keep to these rules, and one draw needn't show every extreme that they name: `lengths`: each sample has at least one token; some sample has 16. `dest`: every learner receives exactly 32 samples; one index of dp sends at most 4 samples to one learner, and exactly 4 to some. The samples of one learner occupy disjoint rows offsets[s] to offsets[s] + lengths[s] - 1 within its 512 rows; some sample starts at row 496.
All inputs are finite; a program needn't handle non-finite values.
Results may differ from the reference program's by a relative error of at most 0.029.
The reference program's roundings to bfloat16 on the way (of `packed`, `probs_b` and `dscore_b`) count: a program that leaves them out, or rounds other values in their place, can miss the bound.
Values may be sent and summed in bfloat16 or wider, within the bound.
No kernel may reach another device: no remote copies, remote signals or barrier semaphores. Data moves between devices by JAX's collectives and lax.ppermute only.
A program may use at most 128 MiB of HBM per device.

```python
import jax
import jax.numpy as jnp
from jax import lax

D = 8192
HEAD_DIM = 128
Q_HEADS = 32
KV_HEADS = 4
LMAX = 16
SAMP_DEV = 32
SAMPLES = 256
ROWS_DEV = 512
ROWS = 4096
KV_COLS = 512
Q_COLS = 4096
N_DP = 8


def route_tables(key):
    shift_key = jax.random.fold_in(key, 11)
    length_key = jax.random.fold_in(key, 12)
    spacing_key = jax.random.fold_in(key, 13)
    order = jax.random.permutation(shift_key, N_DP).astype(jnp.int32)
    column = jnp.arange(SAMP_DEV, dtype=jnp.int32)
    shift = order[column % N_DP]
    anchor = jnp.arange(N_DP, dtype=jnp.int32)
    target = (anchor[:, None] + shift[None, :]) % N_DP
    sizes = jax.random.randint(length_key, (N_DP, SAMP_DEV), 1, LMAX + 1).astype(jnp.int32)
    sizes = sizes.at[0, 0].set(LMAX)
    source = (anchor[:, None] - shift[None, :]) % N_DP
    learner_sizes = sizes[source, column[None, :]]
    spacing = jax.random.randint(spacing_key, (N_DP, SAMP_DEV), 0, LMAX - learner_sizes + 1).astype(jnp.int32)
    spacing = spacing.at[0].set(LMAX - learner_sizes[0])
    stride = learner_sizes + spacing
    starts = jnp.cumsum(stride, axis=1).astype(jnp.int32) - stride
    placed = starts[target, column[None, :]]
    return (target.reshape(-1), sizes.reshape(-1), placed.reshape(-1))


def draw_lengths(key, part):
    return route_tables(key)[1].astype(jnp.int32)


def draw_dest(key, part):
    return route_tables(key)[0].astype(jnp.int32)


def draw_offsets(key, part):
    return route_tables(key)[2].astype(jnp.int32)


def draw_queries(key, part):
    value_key = jax.random.fold_in(key, 21)
    values = jnp.clip(jax.random.normal(value_key, (ROWS, Q_COLS), jnp.float32), -6.0, 6.0)
    return values.astype(jnp.bfloat16)


def block_levels(key, shape, split, smallest, top_value):
    loudness = 1.0
    for dim, blocks in split:
        heights = jax.random.uniform(jax.random.fold_in(jax.random.fold_in(key, 6), dim), (blocks,), jnp.float32, smallest / len(split), top_value / len(split))
        loudness = loudness * jnp.repeat(jnp.exp(heights), shape[dim] // blocks).reshape((-1,) + (1,) * (len(shape) - 1 - dim))
    return loudness


def bell_draw(own_key, shape, width, limit, cuts=(), held_as=jnp.bfloat16):
    array = width * jax.random.normal(own_key, shape, jnp.float32)
    if cuts:
        array = array * block_levels(own_key, shape, cuts, -0.22, 0.18)
    return jnp.clip(array, -limit, limit).astype(held_as)


def setup_inputs(seed: int = 0) -> dict:
    key_of = jax.random.split(jax.random.key(seed), 9)
    return {
        "roll_x": bell_draw(key_of[0], (SAMPLES, LMAX, D), 1.0, 6.0, ((0, 8), (2, 4))),
        "lengths": draw_lengths(jax.random.fold_in(key_of[8], 71), 0),
        "dest": draw_dest(jax.random.fold_in(key_of[8], 71), 0),
        "offsets": draw_offsets(jax.random.fold_in(key_of[8], 71), 0),
        "queries": draw_queries(jax.random.fold_in(key_of[8], 71), 0),
        "out_grad": bell_draw(key_of[5], (ROWS, Q_COLS), 1.0, 6.0, ((0, 8), (1, 4))),
        "w_key": bell_draw(key_of[6], (D, KV_COLS), D ** -0.5, 0.0625, ((0, 4),)),
        "w_value": bell_draw(key_of[7], (D, KV_COLS), D ** -0.5, 0.0625, ((0, 4),)),
    }


def attend(qs, ks, vs, grads, mask):
    scale = 1.0 / (qs.shape[-1] ** 0.5)
    qf = qs.astype(jnp.float32)
    kf = ks.astype(jnp.float32)
    vf = vs.astype(jnp.float32)
    gf = grads.astype(jnp.float32)
    scores = jnp.einsum("bqkge,bmke->bkgqm", qf, kf) * scale
    allowed = mask[:, None, None, :, :]
    scores = jnp.where(allowed, scores, -1e30)
    top = jnp.max(scores, axis=-1, keepdims=True)
    expo = jnp.exp(scores - top)
    total = jnp.sum(expo, axis=-1, keepdims=True)
    probs = jnp.where(allowed, expo / total, 0.0)
    probs_b = probs.astype(jnp.bfloat16)
    out = jnp.einsum("bkgqm,bmke->bqkge", probs_b.astype(jnp.float32), vf).astype(jnp.bfloat16)
    dprob = jnp.einsum("bqkge,bmke->bkgqm", gf, vf)
    delta = jnp.einsum("bqkge,bqkge->bkgq", gf, out.astype(jnp.float32))
    dscore = probs * (dprob - delta[..., None])
    dscore_b = dscore.astype(jnp.bfloat16).astype(jnp.float32)
    key_grad = (jnp.einsum("bkgqm,bqkge->bmke", dscore_b, qf) * scale).astype(jnp.bfloat16)
    val_grad = jnp.einsum("bkgqm,bqkge->bmke", probs_b.astype(jnp.float32), gf).astype(jnp.bfloat16)
    return out, key_grad, val_grad


def reference(roll_x, lengths, dest, offsets, queries, out_grad, w_key, w_value):
    position = jnp.arange(LMAX, dtype=jnp.int32)
    live = position[None, :] < lengths[:, None]
    target = jnp.where(live, dest[:, None] * ROWS_DEV + offsets[:, None] + position[None, :], ROWS).astype(jnp.int32)
    flat = target.reshape(-1)
    packed = jnp.zeros((ROWS, D), jnp.bfloat16).at[flat].set(roll_x.reshape(-1, D), mode="drop")
    sample_ids = jnp.broadcast_to(jnp.arange(SAMPLES, dtype=jnp.int32)[:, None], (SAMPLES, LMAX))
    seg = jnp.full((ROWS,), -1, jnp.int32).at[flat].set(sample_ids.reshape(-1), mode="drop")
    group = Q_HEADS // KV_HEADS
    rowpos = jnp.arange(ROWS_DEV, dtype=jnp.int32)
    causal = rowpos[None, :] <= rowpos[:, None]

    def learner(carry, pieces):
        x_rows, seg_rows, q_rows, g_rows = pieces
        keys = jnp.dot(x_rows, w_key, preferred_element_type=jnp.float32).astype(jnp.bfloat16)
        vals = jnp.dot(x_rows, w_value, preferred_element_type=jnp.float32).astype(jnp.bfloat16)
        mask = (seg_rows[:, None] == seg_rows[None, :]) & (seg_rows[:, None] >= 0) & causal
        out, key_grad, val_grad = attend(
            q_rows.reshape(1, ROWS_DEV, KV_HEADS, group, HEAD_DIM),
            keys.reshape(1, ROWS_DEV, KV_HEADS, HEAD_DIM),
            vals.reshape(1, ROWS_DEV, KV_HEADS, HEAD_DIM),
            g_rows.reshape(1, ROWS_DEV, KV_HEADS, group, HEAD_DIM),
            mask[None])
        key_grad = key_grad.reshape(ROWS_DEV, KV_COLS)
        val_grad = val_grad.reshape(ROWS_DEV, KV_COLS)
        grad_rows = (jnp.dot(key_grad, w_key.T, preferred_element_type=jnp.float32)
                     + jnp.dot(val_grad, w_value.T, preferred_element_type=jnp.float32)).astype(jnp.bfloat16)
        sum_k = carry[0] + jnp.dot(x_rows.T, key_grad, preferred_element_type=jnp.float32)
        sum_v = carry[1] + jnp.dot(x_rows.T, val_grad, preferred_element_type=jnp.float32)
        return (sum_k, sum_v), (out.reshape(ROWS_DEV, Q_COLS), grad_rows)

    start = (jnp.zeros((D, KV_COLS), jnp.float32), jnp.zeros((D, KV_COLS), jnp.float32))
    pieces = (packed.reshape(N_DP, ROWS_DEV, D), seg.reshape(N_DP, ROWS_DEV),
              queries.reshape(N_DP, ROWS_DEV, Q_COLS), out_grad.reshape(N_DP, ROWS_DEV, Q_COLS))
    sums, stacked = lax.scan(learner, start, pieces)
    attn_out = stacked[0].reshape(ROWS, Q_COLS)
    grad_x = stacked[1].reshape(ROWS, D)
    return attn_out, grad_x, sums[0] / N_DP, sums[1] / N_DP
```

```python
import functools

import jax
import jax.numpy as jnp
from jax import lax
from jax.experimental import pallas as pl
from jax.experimental.pallas import tpu as pltpu
from jax.sharding import PartitionSpec as P

HEAD_DIM = 128


def attend(qs, ks, vs, grads, mask):
    scale = 1.0 / qs.shape[-1] ** 0.5
    scores = jnp.einsum("bqkge,bmke->bkgqm", qs, ks, preferred_element_type=jnp.float32) * scale
    allowed = mask[:, None, None, :, :]
    scores = jnp.where(allowed, scores, -1e30)
    top = jnp.max(scores, axis=-1, keepdims=True)
    expo = jnp.exp(scores - top)
    total = jnp.sum(expo, axis=-1, keepdims=True)
    probs = jnp.where(allowed, expo / total, 0.0)
    probs_b = probs.astype(jnp.bfloat16)
    out = jnp.einsum("bkgqm,bmke->bqkge", probs_b, vs, preferred_element_type=jnp.float32).astype(
        jnp.bfloat16
    )
    dprob = jnp.einsum("bqkge,bmke->bkgqm", grads, vs, preferred_element_type=jnp.float32)
    delta = jnp.einsum("bqkge,bqkge->bkgq", grads, out, preferred_element_type=jnp.float32)
    dscore = probs * (dprob - delta[..., None])
    dscore_b = dscore.astype(jnp.bfloat16)
    key_grad = (
        jnp.einsum("bkgqm,bqkge->bmke", dscore_b, qs, preferred_element_type=jnp.float32) * scale
    ).astype(jnp.bfloat16)
    val_grad = jnp.einsum(
        "bkgqm,bqkge->bmke", probs_b, grads, preferred_element_type=jnp.float32
    ).astype(jnp.bfloat16)
    return (out, key_grad, val_grad)


def input_grads(key_all, val_all, w_key, w_value):
    contract = (((1,), (1,)), ((), ()))
    total = lax.dot_general(key_all, w_key, contract, preferred_element_type=jnp.float32)
    total = total + lax.dot_general(val_all, w_value, contract, preferred_element_type=jnp.float32)
    return total.astype(jnp.bfloat16)


def general(roll_x, lengths, dest, offsets, queries, out_grad, w_key, w_value):
    learners = lax.axis_size("dp")
    samp, lmax, feats = roll_x.shape
    rows = queries.shape[0]
    slots_per = (samp + learners - 1) // learners
    slot_count = learners * slots_per
    order = jnp.arange(samp, dtype=jnp.int32)
    earlier = (dest[None, :] == dest[:, None]) & (order[None, :] < order[:, None])
    rank = jnp.sum(earlier.astype(jnp.int32), axis=1)
    slot = dest * slots_per + rank
    match = slot[None, :] == jnp.arange(slot_count, dtype=jnp.int32)[:, None]
    filled = jnp.any(match, axis=1)
    pick = jnp.sum(jnp.where(match, order[None, :], 0), axis=1)
    send_x = jnp.where(
        filled[:, None, None], jnp.take(roll_x, pick, axis=0), jnp.zeros((), jnp.bfloat16)
    )
    send_len = jnp.where(filled, jnp.take(lengths, pick), 0)
    send_off = jnp.where(filled, jnp.take(offsets, pick), 0)
    recv_x, recv_len, recv_off = (
        lax.all_to_all(send_x, "dp", split_axis=0, concat_axis=0, tiled=True),
        lax.all_to_all(send_len, "dp", split_axis=0, concat_axis=0, tiled=True),
        lax.all_to_all(send_off, "dp", split_axis=0, concat_axis=0, tiled=True),
    )
    position = jnp.arange(lmax, dtype=jnp.int32)
    live = position[None, :] < recv_len[:, None]
    target = jnp.where(live, recv_off[:, None] + position[None, :], rows).astype(jnp.int32)
    flat = target.reshape(-1)
    packed = (
        jnp.zeros((rows, feats), jnp.bfloat16).at[flat].set(recv_x.reshape(-1, feats), mode="drop")
    )
    part_k = jnp.dot(packed, w_key, preferred_element_type=jnp.float32)
    part_v = jnp.dot(packed, w_value, preferred_element_type=jnp.float32)
    key_mine, val_mine = (
        lax.psum_scatter(part_k, "mp", scatter_dimension=1, tiled=True),
        lax.psum_scatter(part_v, "mp", scatter_dimension=1, tiled=True),
    )
    keys = key_mine.astype(jnp.bfloat16)
    vals = val_mine.astype(jnp.bfloat16)
    local_heads = keys.shape[1] // HEAD_DIM
    q_cols = queries.shape[1]
    group = q_cols // (local_heads * HEAD_DIM)
    slot_ids = jnp.broadcast_to(
        jnp.arange(slot_count, dtype=jnp.int32)[:, None], (slot_count, lmax)
    )
    seg = jnp.full((rows,), -1, jnp.int32).at[flat].set(slot_ids.reshape(-1), mode="drop")
    rowpos = jnp.arange(rows, dtype=jnp.int32)
    mask = (
        (seg[:, None] == seg[None, :]) & (seg[:, None] >= 0) & (rowpos[None, :] <= rowpos[:, None])
    )
    out, key_grad, val_grad = attend(
        queries.reshape(1, rows, local_heads, group, HEAD_DIM),
        keys.reshape(1, rows, local_heads, HEAD_DIM),
        vals.reshape(1, rows, local_heads, HEAD_DIM),
        out_grad.reshape(1, rows, local_heads, group, HEAD_DIM),
        mask[None],
    )
    attn_out = out.reshape(rows, q_cols)
    key_grad = key_grad.reshape(rows, local_heads * HEAD_DIM)
    val_grad = val_grad.reshape(rows, local_heads * HEAD_DIM)
    key_all, val_all = (
        lax.all_gather(key_grad, "mp", axis=1, tiled=True),
        lax.all_gather(val_grad, "mp", axis=1, tiled=True),
    )
    grad_x = input_grads(key_all, val_all, w_key, w_value)
    contract = (((0,), (0,)), ((), ()))
    whole_k = lax.dot_general(packed, key_all, contract, preferred_element_type=jnp.float32)
    whole_v = lax.dot_general(packed, val_all, contract, preferred_element_type=jnp.float32)
    sum_k, sum_v = (
        lax.psum_scatter(whole_k, "dp", scatter_dimension=0, tiled=True),
        lax.psum_scatter(whole_v, "dp", scatter_dimension=0, tiled=True),
    )
    return (attn_out, grad_x, sum_k / learners, sum_v / learners)


BF16, F32, I32 = jnp.bfloat16, jnp.float32, jnp.int32
ROWS_LAST = (((0,), (0,)), ((), ()))
COLS_LAST = (((1,), (1,)), ((), ()))


def dot(a, b, dims=(((1,), (0,)), ((), ()))):
    return lax.dot_general(a, b, dims, preferred_element_type=F32)


def iota(shape, dim):
    return lax.broadcasted_iota(I32, shape, dim)


def params(steps=1):
    return pltpu.CompilerParams(
        dimension_semantics=("arbitrary",) * steps, vmem_limit_bytes=48 * 1024 * 1024
    )


def cost(flops, moved):
    return pl.CostEstimate(flops=flops, bytes_accessed=moved, transcendentals=0)


def whole(shape):
    zeros = (0,) * len(shape)
    return pl.BlockSpec(shape, lambda *_: zeros)


def project_kernel(me_ref, x_ref, wk_ref, wv_ref, out_ref):
    weights = jnp.concatenate([wk_ref[...], wv_ref[...]], axis=1)
    out_ref[0] = dot(x_ref[...], weights)


def project(me, x, w_key, w_value, first):
    rows, feats = x.shape
    spec = pltpu.PrefetchScalarGridSpec(
        num_scalar_prefetch=1,
        grid=(2,),
        in_specs=[
            pl.BlockSpec((rows, feats), lambda i, me: (0, 0)),
            pl.BlockSpec((feats, HEAD_DIM), lambda i, me: (0, me[0] ^ (first - 2 * i))),
            pl.BlockSpec((feats, HEAD_DIM), lambda i, me: (0, me[0] ^ (first - 2 * i))),
        ],
        out_specs=pl.BlockSpec((1, rows, 2 * HEAD_DIM), lambda i, me: (i, 0, 0)),
    )
    return pl.pallas_call(
        project_kernel,
        out_shape=jax.ShapeDtypeStruct((2, rows, 2 * HEAD_DIM), F32),
        grid_spec=spec,
        compiler_params=params(),
        cost_estimate=cost(4 * rows * feats * 2 * HEAD_DIM, 6 << 20),
        name="project",
    )(me, x, w_key, w_value)


def slots_kernel(per, dest_ref, len_ref, off_ref, x_ref, xs_ref, pick_ref, meta_ref, pick):
    samp = dest_ref.shape[1]
    rows = x_ref.shape[0]
    lmax = rows // samp

    @pl.when(pl.program_id(0) == 0)
    def _():
        row = dest_ref[...]
        a, b = iota((samp, samp), 0), iota((samp, samp), 1)
        col = jnp.sum(jnp.where(a == b, row, 0), axis=1, keepdims=True)
        rank = jnp.sum(jnp.where((col == row) & (a < b), 1, 0), axis=0, keepdims=True)
        slot = row * per + rank
        a, b = iota((samp, rows), 0), iota((samp, rows), 1)
        spread = (a == lax.div(b, lmax)).astype(BF16)
        wide = dot(jnp.broadcast_to(slot, (8, samp)).astype(BF16), spread)[0:1]
        source = wide.astype(I32) * lmax + lax.rem(iota((1, rows), 1), lmax)
        pick[...] = (iota((rows, rows), 0) == source).astype(BF16)
        pick_ref[...] = pick[...]
        held = iota((samp, samp), 0) == slot
        size = jnp.sum(jnp.where(held, len_ref[...], 0), axis=1, keepdims=True)
        start = jnp.sum(jnp.where(held, off_ref[...], 0), axis=1, keepdims=True)
        lane = iota((samp, meta_ref.shape[2]), 1)
        table = jnp.where(
            lane == 0, size, jnp.where(lane == 1, lax.div(start, lmax), jnp.where(lane == 2, lax.rem(start, lmax), 0))
        ).astype(BF16)
        lines = meta_ref.shape[0] * meta_ref.shape[1]
        a, b = iota((lines, samp), 0), iota((lines, samp), 1)
        place = ((b == lax.div(a, 16) * per + lax.rem(a, 16)) & (lax.rem(a, 16) < per)).astype(BF16)
        meta_ref[...] = dot(place, table).astype(BF16).reshape(meta_ref.shape)

    xs_ref[0] = dot(pick[...], x_ref[...]).astype(BF16)


def slots(dest, lengths, offsets, x, learners, per):
    rows, feats = x.shape
    samp = dest.shape[0]
    part = feats // learners
    line = whole((1, samp))
    return pl.pallas_call(
        functools.partial(slots_kernel, per),
        out_shape=(
            jax.ShapeDtypeStruct((learners, rows, part), BF16),
            jax.ShapeDtypeStruct((rows, rows), BF16),
            jax.ShapeDtypeStruct((learners, 16, 2 * HEAD_DIM), BF16),
        ),
        grid=(learners,),
        in_specs=[line, line, line, pl.BlockSpec((rows, part), lambda i: (0, i))],
        out_specs=(
            pl.BlockSpec((1, rows, part), lambda i: (i, 0, 0)),
            whole((rows, rows)),
            whole((learners, 16, 2 * HEAD_DIM)),
        ),
        scratch_shapes=[pltpu.VMEM((rows, rows), BF16)],
        compiler_params=params(),
        cost_estimate=cost(2 * rows * rows * feats, 5 << 20),
        name="slots",
    )(dest.reshape(1, samp), lengths.reshape(1, samp), offsets.reshape(1, samp), x)


def pack_kernel(mine_ref, core_ref, across_ref, pick_ref, meta_ref, out_ref):
    total = (mine_ref[0] + core_ref[0]) + across_ref[...]
    placed = dot(pick_ref[...], total.astype(BF16)).astype(BF16)
    learners = out_ref.shape[0]
    block = placed.shape[0] // learners
    for i in range(learners):
        out_ref[i, :block, :] = placed[i * block : (i + 1) * block]
        out_ref[i, block:, :] = meta_ref[i]


def pack(mine, core, across, pick, meta):
    rows, cols = across.shape
    learners, extra, _ = meta.shape
    out = (learners, rows // learners + extra, cols)
    second = pl.BlockSpec((1, rows, cols), lambda i: (1, 0, 0))
    return pl.pallas_call(
        pack_kernel,
        out_shape=jax.ShapeDtypeStruct(out, BF16),
        grid=(1,),
        in_specs=[second, second, whole((rows, cols)), whole((rows, rows)), whole(meta.shape)],
        out_specs=whole(out),
        compiler_params=params(),
        cost_estimate=cost(2 * rows * rows * cols, 3 << 20),
        name="pack",
    )(mine, core, across, pick, meta)


def attention_kernel(lmax, per, kv_ref, q_ref, g_ref, out_ref, grad_ref, place_ref, slot_out):
    rows, cols = q_ref.shape
    learners, lines, _ = kv_ref.shape
    block = rows // learners
    heads = cols // HEAD_DIM
    scale = 1.0 / HEAD_DIM**0.5
    meta = kv_ref[:, block:, :HEAD_DIM].reshape(learners * (lines - block), HEAD_DIM)
    a, b = iota((rows, meta.shape[0]), 0), iota((rows, meta.shape[0]), 1)
    spread = (lax.div(a, block) * (lines - block) + lax.div(lax.rem(a, block), lmax) == b).astype(BF16)
    table = dot(spread, meta).astype(I32)
    inner = lax.rem(iota((rows, 1), 0), lmax)
    alive = inner < table[:, 0:1]
    target = jnp.where(alive, table[:, 1:2] * lmax + table[:, 2:3] + inner, -1)
    place_ref[...] = (iota((rows, rows), 1) == target).astype(BF16)
    size = HEAD_DIM
    a, b = iota((size, size), 0), iota((size, size), 1)
    near = (lax.div(a, lmax) == lax.div(b, lmax)) & (b <= a)
    for i in range(rows // size):
        span = slice(i * size, (i + 1) * size)
        first = i * size // block
        kv = jnp.concatenate([kv_ref[first + j, :block, :] for j in range(size // block)], axis=0)
        k, v = kv[:, :HEAD_DIM], kv[:, HEAD_DIM:]
        place = place_ref[span, :]
        q = dot(place, q_ref[...]).astype(BF16)
        g = dot(place, g_ref[...]).astype(BF16)
        q = jnp.concatenate([q[:, h * HEAD_DIM : (h + 1) * HEAD_DIM] for h in range(heads)], axis=0)
        g = jnp.concatenate([g[:, h * HEAD_DIM : (h + 1) * HEAD_DIM] for h in range(heads)], axis=0)
        allowed = jnp.tile(near & alive[span], (heads, 1))
        scores = jnp.where(allowed, dot(q, k, COLS_LAST) * scale, -1e30)
        top = jnp.max(scores, axis=1, keepdims=True)
        expo = jnp.exp(scores - top)
        total = jnp.sum(expo, axis=1, keepdims=True)
        probs = jnp.where(allowed, expo / total, 0.0)
        probs_b = probs.astype(BF16)
        out = dot(probs_b, v).astype(BF16)
        dprob = dot(g, v, COLS_LAST)
        delta = jnp.sum(g.astype(F32) * out.astype(F32), axis=1, keepdims=True)
        dscore_b = (probs * (dprob - delta)).astype(BF16)
        grad_ref[span, :HEAD_DIM] = (dot(dscore_b, q, ROWS_LAST) * scale).astype(BF16)
        grad_ref[span, HEAD_DIM:] = dot(probs_b, g, ROWS_LAST).astype(BF16)
        for h in range(heads):
            slot_out[span, h * HEAD_DIM : (h + 1) * HEAD_DIM] = out[h * size : (h + 1) * size]
    out_ref[...] = dot(place_ref[...], slot_out[...], ROWS_LAST).astype(BF16)


def attention(kv, queries, out_grad, lmax, per):
    rows, cols = queries.shape
    return pl.pallas_call(
        functools.partial(attention_kernel, lmax, per),
        out_shape=(
            jax.ShapeDtypeStruct((rows, cols), BF16),
            jax.ShapeDtypeStruct((rows, 2 * HEAD_DIM), BF16),
            jax.ShapeDtypeStruct((rows, rows), BF16),
        ),
        grid=(1,),
        in_specs=[whole(kv.shape), whole((rows, cols)), whole((rows, cols))],
        out_specs=(whole((rows, cols)), whole((rows, 2 * HEAD_DIM)), whole((rows, rows))),
        scratch_shapes=[pltpu.VMEM((rows, cols), BF16)],
        compiler_params=params(),
        cost_estimate=cost(8 * rows * rows * cols, 4 << 20),
        name="attention",
    )(kv, queries, out_grad)


def rows_kernel(me_ref, place_ref, g0, g1, g2, g3, wk_ref, wv_ref, out_ref, grads):
    @pl.when(pl.program_id(0) == 0)
    def _():
        half = grads.shape[1] // 2
        for i, ref in enumerate((g0, g1, g2, g3)):
            part = dot(place_ref[...], ref[...], ROWS_LAST).astype(BF16)
            at = pl.multiple_of((me_ref[0] ^ i) * HEAD_DIM, HEAD_DIM)
            grads[:, pl.ds(at, HEAD_DIM)] = part[:, :HEAD_DIM]
            grads[:, pl.ds(at + half, HEAD_DIM)] = part[:, HEAD_DIM:]

    half = grads.shape[1] // 2
    total = dot(grads[:, :half], wk_ref[...], COLS_LAST)
    out_ref[...] = (total + dot(grads[:, half:], wv_ref[...], COLS_LAST)).astype(BF16)


def row_grads(me, place, parts, w_key, w_value):
    feats, cols = w_key.shape
    rows = place.shape[0]
    step = 512
    spec = pltpu.PrefetchScalarGridSpec(
        num_scalar_prefetch=1,
        grid=(feats // step,),
        in_specs=[whole((rows, rows))]
        + [whole((rows, 2 * HEAD_DIM))] * 4
        + [pl.BlockSpec((step, cols), lambda i, me: (i, 0))] * 2,
        out_specs=pl.BlockSpec((rows, step), lambda i, me: (0, i)),
        scratch_shapes=[pltpu.VMEM((rows, 2 * cols), BF16)],
    )
    return pl.pallas_call(
        rows_kernel,
        out_shape=jax.ShapeDtypeStruct((rows, feats), BF16),
        grid_spec=spec,
        compiler_params=params(),
        cost_estimate=cost(4 * rows * feats * cols, 8 << 20),
        name="row_grads",
    )(me, place, *parts, w_key, w_value)


def weights_kernel(codes, starts, me_ref, *refs):
    refs = list(refs)
    x_refs = refs[:2]
    g_refs = refs[2 : 2 + len(codes)]
    before = refs[2 + len(codes)] if starts else None
    out_ref = refs[-1]
    learners, rows, part = x_refs[0].shape
    block = rows // learners
    for side in range(2):
        for far in range(2):
            mine = [(e, r) for (e, f), r in zip(codes, g_refs) if f == far]
            if not mine:
                continue
            cols = slice(far * 2 * HEAD_DIM, (far + 1) * 2 * HEAD_DIM)
            total = before[side, :, cols] if starts else None
            for code, ref in mine:
                at = pl.multiple_of((me_ref[0] ^ code) * block, block)
                x = x_refs[side][:, pl.ds(at, block), :].reshape(rows, part)
                term = dot(x, ref[...], ROWS_LAST)
                total = term if total is None else total + term
            out_ref[side, :, cols] = total


def weight_grads(me, x, x_core, pieces, before=None):
    codes = list(pieces)
    learners, rows, part = x.shape
    shape = (2, part, 4 * HEAD_DIM)
    given = [x, x_core] + [pieces[c] for c in codes] + ([] if before is None else [before])
    spec = pltpu.PrefetchScalarGridSpec(
        num_scalar_prefetch=1,
        grid=(1,),
        in_specs=[whole(a.shape) for a in given],
        out_specs=whole(shape),
    )
    return pl.pallas_call(
        functools.partial(weights_kernel, codes, before is not None),
        out_shape=jax.ShapeDtypeStruct(shape, F32),
        grid_spec=spec,
        compiler_params=params(),
        cost_estimate=cost(4 * len(codes) * rows * part * 2 * HEAD_DIM, 6 << 20),
        name="weight_grads",
    )(me, *given)


def finish_kernel(learners, me_ref, own_ref, core_ref, k_ref, v_ref):
    for side, ref in enumerate((own_ref, core_ref)):
        for far in range(2):
            at = pl.multiple_of((me_ref[0] ^ (side + 2 * far)) * HEAD_DIM, HEAD_DIM)
            base = far * 2 * HEAD_DIM
            k_ref[:, pl.ds(at, HEAD_DIM)] = ref[0, :, base : base + HEAD_DIM] / learners
            v_ref[:, pl.ds(at, HEAD_DIM)] = ref[0, :, base + HEAD_DIM : base + 2 * HEAD_DIM] / learners


def finish(me, own, core, learners):
    _, part, cols = own.shape
    spec = pltpu.PrefetchScalarGridSpec(
        num_scalar_prefetch=1,
        grid=(1,),
        in_specs=[whole((1, part, cols))] * 2,
        out_specs=(whole((part, cols)),) * 2,
    )
    return pl.pallas_call(
        functools.partial(finish_kernel, float(learners)),
        out_shape=(jax.ShapeDtypeStruct((part, cols), F32),) * 2,
        grid_spec=spec,
        compiler_params=params(),
        cost_estimate=cost(part * cols, 2 << 20),
        name="finish",
    )(me, own, core)


def swap(x, axis, code):
    return lax.ppermute(x, axis, [(i, i ^ code) for i in range(lax.axis_size(axis))])


def local(roll_x, lengths, dest, offsets, queries, out_grad, w_key, w_value):
    learners = lax.axis_size("dp")
    samp, lmax, feats = roll_x.shape
    per = (samp + learners - 1) // learners
    x = roll_x.reshape(samp * lmax, feats)
    m = lax.axis_index("mp").astype(I32).reshape(1)
    d = lax.axis_index("dp").astype(I32).reshape(1)

    away = project(m, x, w_key, w_value, 3)
    core = swap(away, "mp", 1)
    mine = project(m, x, w_key, w_value, 2)
    across = swap(mine[0] + core[0], "mp", 2)
    xs, pick, meta = slots(dest, lengths, offsets, x, learners, per)
    xs = lax.all_to_all(xs, "dp", split_axis=0, concat_axis=0, tiled=True)
    xs_core = swap(xs, "mp", 1)
    kv = pack(mine, core, across, pick, meta)
    kv = lax.all_to_all(kv, "dp", split_axis=0, concat_axis=0, tiled=True)

    attn_out, grads, place = attention(kv, queries, out_grad, lmax, per)

    near = {(0, 0): grads}
    hops = [
        ((0, 0), "dp", 4), ((0, 0), "dp", 2), ((0, 0), "mp", 2), ((0, 0), "dp", 1),
        ((0, 1), "dp", 4), ((1, 0), "dp", 2), ((1, 0), "mp", 2),
        ((2, 0), "mp", 2), ((4, 0), "dp", 1), ((4, 0), "dp", 2), ((3, 0), "mp", 2),
        ((5, 0), "mp", 2), ((6, 0), "dp", 1), ((4, 1), "dp", 2), ((6, 1), "dp", 1),
    ]
    for (code, far), axis, step in hops:
        key = (code ^ step, far) if axis == "dp" else (code, 1 - far)
        near[key] = swap(near[code, far], axis, step)
    grad_x = row_grads(
        m,
        place,
        [near[0, 0], swap(near[0, 0], "mp", 1), near[0, 1], swap(near[0, 1], "mp", 1)],
        w_key,
        w_value,
    )
    early = [(0, 0), (0, 1), (1, 0), (1, 1), (2, 0), (4, 0), (2, 1), (3, 0), (3, 1), (5, 0), (4, 1)]
    sums = weight_grads(d, xs, xs_core, {c: near[c] for c in early})
    sums = weight_grads(d, xs, xs_core, {c: near[c] for c in near if c not in early}, sums)
    grad_wk, grad_wv = finish(m, sums, swap(sums[1:], "mp", 1), learners)
    return (attn_out, grad_x, grad_wk, grad_wv)


def solution(mesh):
    dp, mp = mesh.shape["dp"], mesh.shape["mp"]
    body = local if dp == 8 and mp == 4 else general
    return jax.shard_map(
        body,
        mesh=mesh,
        in_specs=(
            P("dp", None, "mp"),
            P("dp"),
            P("dp"),
            P("dp"),
            P("dp", "mp"),
            P("dp", "mp"),
            P("mp", None),
            P("mp", None),
        ),
        out_specs=(P("dp", "mp"), P("dp", "mp"), P(("mp", "dp"), None), P(("mp", "dp"), None)),
        check_vma=False,
    )
```

```python
import functools

import jax
import jax.numpy as jnp
from jax import lax
from jax.experimental import pallas as pl
from jax.experimental.pallas import tpu as pltpu
from jax.sharding import PartitionSpec as P

HEAD_DIM = 128


def attend(qs, ks, vs, grads, mask):
    scale = 1.0 / qs.shape[-1] ** 0.5
    scores = jnp.einsum("bqkge,bmke->bkgqm", qs, ks, preferred_element_type=jnp.float32) * scale
    allowed = mask[:, None, None, :, :]
    scores = jnp.where(allowed, scores, -1e30)
    top = jnp.max(scores, axis=-1, keepdims=True)
    expo = jnp.exp(scores - top)
    total = jnp.sum(expo, axis=-1, keepdims=True)
    probs = jnp.where(allowed, expo / total, 0.0)
    probs_b = probs.astype(jnp.bfloat16)
    out = jnp.einsum("bkgqm,bmke->bqkge", probs_b, vs, preferred_element_type=jnp.float32).astype(
        jnp.bfloat16
    )
    dprob = jnp.einsum("bqkge,bmke->bkgqm", grads, vs, preferred_element_type=jnp.float32)
    delta = jnp.einsum("bqkge,bqkge->bkgq", grads, out, preferred_element_type=jnp.float32)
    dscore = probs * (dprob - delta[..., None])
    dscore_b = dscore.astype(jnp.bfloat16)
    key_grad = (
        jnp.einsum("bkgqm,bqkge->bmke", dscore_b, qs, preferred_element_type=jnp.float32) * scale
    ).astype(jnp.bfloat16)
    val_grad = jnp.einsum(
        "bkgqm,bqkge->bmke", probs_b, grads, preferred_element_type=jnp.float32
    ).astype(jnp.bfloat16)
    return (out, key_grad, val_grad)


def input_grads(key_all, val_all, w_key, w_value):
    contract = (((1,), (1,)), ((), ()))
    total = lax.dot_general(key_all, w_key, contract, preferred_element_type=jnp.float32)
    total = total + lax.dot_general(val_all, w_value, contract, preferred_element_type=jnp.float32)
    return total.astype(jnp.bfloat16)


def general(roll_x, lengths, dest, offsets, queries, out_grad, w_key, w_value):
    learners = lax.axis_size("dp")
    samp, lmax, feats = roll_x.shape
    rows = queries.shape[0]
    slots_per = (samp + learners - 1) // learners
    slot_count = learners * slots_per
    order = jnp.arange(samp, dtype=jnp.int32)
    earlier = (dest[None, :] == dest[:, None]) & (order[None, :] < order[:, None])
    rank = jnp.sum(earlier.astype(jnp.int32), axis=1)
    slot = dest * slots_per + rank
    match = slot[None, :] == jnp.arange(slot_count, dtype=jnp.int32)[:, None]
    filled = jnp.any(match, axis=1)
    pick = jnp.sum(jnp.where(match, order[None, :], 0), axis=1)
    send_x = jnp.where(
        filled[:, None, None], jnp.take(roll_x, pick, axis=0), jnp.zeros((), jnp.bfloat16)
    )
    send_len = jnp.where(filled, jnp.take(lengths, pick), 0)
    send_off = jnp.where(filled, jnp.take(offsets, pick), 0)
    recv_x, recv_len, recv_off = (
        lax.all_to_all(send_x, "dp", split_axis=0, concat_axis=0, tiled=True),
        lax.all_to_all(send_len, "dp", split_axis=0, concat_axis=0, tiled=True),
        lax.all_to_all(send_off, "dp", split_axis=0, concat_axis=0, tiled=True),
    )
    position = jnp.arange(lmax, dtype=jnp.int32)
    live = position[None, :] < recv_len[:, None]
    target = jnp.where(live, recv_off[:, None] + position[None, :], rows).astype(jnp.int32)
    flat = target.reshape(-1)
    packed = (
        jnp.zeros((rows, feats), jnp.bfloat16).at[flat].set(recv_x.reshape(-1, feats), mode="drop")
    )
    part_k = jnp.dot(packed, w_key, preferred_element_type=jnp.float32)
    part_v = jnp.dot(packed, w_value, preferred_element_type=jnp.float32)
    key_mine, val_mine = (
        lax.psum_scatter(part_k, "mp", scatter_dimension=1, tiled=True),
        lax.psum_scatter(part_v, "mp", scatter_dimension=1, tiled=True),
    )
    keys = key_mine.astype(jnp.bfloat16)
    vals = val_mine.astype(jnp.bfloat16)
    local_heads = keys.shape[1] // HEAD_DIM
    q_cols = queries.shape[1]
    group = q_cols // (local_heads * HEAD_DIM)
    slot_ids = jnp.broadcast_to(
        jnp.arange(slot_count, dtype=jnp.int32)[:, None], (slot_count, lmax)
    )
    seg = jnp.full((rows,), -1, jnp.int32).at[flat].set(slot_ids.reshape(-1), mode="drop")
    rowpos = jnp.arange(rows, dtype=jnp.int32)
    mask = (
        (seg[:, None] == seg[None, :]) & (seg[:, None] >= 0) & (rowpos[None, :] <= rowpos[:, None])
    )
    out, key_grad, val_grad = attend(
        queries.reshape(1, rows, local_heads, group, HEAD_DIM),
        keys.reshape(1, rows, local_heads, HEAD_DIM),
        vals.reshape(1, rows, local_heads, HEAD_DIM),
        out_grad.reshape(1, rows, local_heads, group, HEAD_DIM),
        mask[None],
    )
    attn_out = out.reshape(rows, q_cols)
    key_grad = key_grad.reshape(rows, local_heads * HEAD_DIM)
    val_grad = val_grad.reshape(rows, local_heads * HEAD_DIM)
    key_all, val_all = (
        lax.all_gather(key_grad, "mp", axis=1, tiled=True),
        lax.all_gather(val_grad, "mp", axis=1, tiled=True),
    )
    grad_x = input_grads(key_all, val_all, w_key, w_value)
    contract = (((0,), (0,)), ((), ()))
    whole_k = lax.dot_general(packed, key_all, contract, preferred_element_type=jnp.float32)
    whole_v = lax.dot_general(packed, val_all, contract, preferred_element_type=jnp.float32)
    sum_k, sum_v = (
        lax.psum_scatter(whole_k, "dp", scatter_dimension=0, tiled=True),
        lax.psum_scatter(whole_v, "dp", scatter_dimension=0, tiled=True),
    )
    return (attn_out, grad_x, sum_k / learners, sum_v / learners)


BF16, F32, I32 = jnp.bfloat16, jnp.float32, jnp.int32
ROWS_LAST = (((0,), (0,)), ((), ()))
COLS_LAST = (((1,), (1,)), ((), ()))


def dot(a, b, dims=(((1,), (0,)), ((), ()))):
    return lax.dot_general(a, b, dims, preferred_element_type=F32)


def iota(shape, dim):
    return lax.broadcasted_iota(I32, shape, dim)


def params(mib=44):
    return pltpu.CompilerParams(
        dimension_semantics=("arbitrary",), vmem_limit_bytes=mib * 1024 * 1024
    )


def cost(flops, moved):
    return pl.CostEstimate(flops=flops, bytes_accessed=moved, transcendentals=0)


def whole(shape):
    zeros = (0,) * len(shape)
    return pl.BlockSpec(shape, lambda *_: zeros)


def project_kernel(me_ref, x_ref, wk_ref, wv_ref, away_ref, mine_ref):
    x = x_ref[...]
    for q in range(4):
        at = pl.ds(pl.multiple_of((me_ref[0] ^ q) * HEAD_DIM, HEAD_DIM), HEAD_DIM)
        term = dot(x, jnp.concatenate([wk_ref[:, at], wv_ref[:, at]], axis=1))
        ref = (away_ref if q % 2 else mine_ref).at[q // 2]

        @pl.when(pl.program_id(0) == 0)
        def _(ref=ref, term=term):
            ref[...] = term

        @pl.when(pl.program_id(0) != 0)
        def _(ref=ref, term=term):
            ref[...] += term


def project(me, x, w_key, w_value):
    rows, feats = x.shape
    cols = w_key.shape[1]
    out = (2, rows, 2 * HEAD_DIM)
    step = 512
    spec = pltpu.PrefetchScalarGridSpec(
        num_scalar_prefetch=1,
        grid=(feats // step,),
        in_specs=[
            pl.BlockSpec((rows, step), lambda i, me: (0, i)),
            pl.BlockSpec((step, cols), lambda i, me: (i, 0)),
            pl.BlockSpec((step, cols), lambda i, me: (i, 0)),
        ],
        out_specs=(whole(out), whole(out)),
    )
    return pl.pallas_call(
        project_kernel,
        out_shape=(jax.ShapeDtypeStruct(out, F32),) * 2,
        grid_spec=spec,
        compiler_params=params(60),
        cost_estimate=cost(4 * rows * feats * cols, 10 << 20),
        name="project",
    )(me, x, w_key, w_value)


def slots_kernel(per, me_ref, dest_ref, len_ref, off_ref, x_ref, *refs):
    *xs_refs, pick_ref, meta_ref = refs
    samp = dest_ref.shape[1]
    rows, feats = x_ref.shape
    lmax = rows // samp
    row = dest_ref[...]
    a, b = iota((samp, samp), 0), iota((samp, samp), 1)
    col = jnp.sum(jnp.where(a == b, row, 0), axis=1, keepdims=True)
    rank = jnp.sum(jnp.where((col == row) & (a < b), 1, 0), axis=0, keepdims=True)
    slot = (row ^ me_ref[0]) * per + rank
    a, b = iota((samp, rows), 0), iota((samp, rows), 1)
    spread = (a == lax.div(b, lmax)).astype(BF16)
    wide = dot(jnp.broadcast_to(slot, (8, samp)).astype(BF16), spread)[0:1]
    source = wide.astype(I32) * lmax + lax.rem(iota((1, rows), 1), lmax)
    pick_ref[...] = (iota((rows, rows), 0) == source).astype(BF16)
    held = iota((samp, samp), 0) == slot
    size = jnp.sum(jnp.where(held, len_ref[...], 0), axis=1, keepdims=True)
    start = jnp.sum(jnp.where(held, off_ref[...], 0), axis=1, keepdims=True)
    lane = iota((samp, meta_ref.shape[2]), 1)
    table = jnp.where(lane == 0, size, jnp.where(lane == 2, lax.rem(start, lmax), 0))
    table = jnp.where(lane == 1, lax.div(start, lmax), table).astype(BF16)
    lines = meta_ref.shape[0] * meta_ref.shape[1]
    a, b = iota((lines, samp), 0), iota((lines, samp), 1)
    place = (b == lax.div(a, 16) * per + lax.rem(a, 16)) & (lax.rem(a, 16) < per)
    meta_ref[...] = dot(place.astype(BF16), table).astype(BF16).reshape(meta_ref.shape)
    part = xs_refs[0].shape[2]
    for f, ref in enumerate(xs_refs):
        for h in range(2):
            at = pl.multiple_of((me_ref[0] ^ (f + h * len(xs_refs))) * part, part)
            ref[h] = dot(pick_ref[...], x_ref[:, pl.ds(at, part)]).astype(BF16)


def slots(me, dest, lengths, offsets, x, learners, per):
    rows, feats = x.shape
    samp = dest.shape[0]
    part = feats // learners
    line = whole((1, samp))
    xs = ((2, rows, part),) * (learners // 2)
    outs = xs + ((rows, rows), (learners, 16, 2 * HEAD_DIM))
    spec = pltpu.PrefetchScalarGridSpec(
        num_scalar_prefetch=1,
        grid=(1,),
        in_specs=[line, line, line, whole((rows, feats))],
        out_specs=tuple(whole(o) for o in outs),
    )
    return pl.pallas_call(
        functools.partial(slots_kernel, per),
        out_shape=tuple(jax.ShapeDtypeStruct(o, BF16) for o in outs),
        grid_spec=spec,
        compiler_params=params(),
        cost_estimate=cost(2 * rows * rows * feats, 5 << 20),
        name="slots",
    )(me, dest.reshape(1, samp), lengths.reshape(1, samp), offsets.reshape(1, samp), x)


def pack_kernel(me_ref, mine_ref, core_ref, across_ref, pick_ref, meta_ref, *out_refs):
    total = (mine_ref[0] + core_ref[0]) + across_ref[...]
    placed = dot(pick_ref[...], total.astype(BF16)).astype(BF16)
    learners = meta_ref.shape[0]
    block = placed.shape[0] // learners
    for i in range(learners):
        ref = out_refs[0].at[me_ref[0] ^ i]
        ref[:block, :] = placed[i * block : (i + 1) * block]
        ref[block:, :] = meta_ref[i]


def pack(me, mine, core, across, pick, meta):
    rows, cols = across.shape
    learners, extra, _ = meta.shape
    out = (rows // learners + extra, cols)
    outs = ((learners,) + out,)
    second = pl.BlockSpec((1, rows, cols), lambda *_: (0, 0, 0))
    spec = pltpu.PrefetchScalarGridSpec(
        num_scalar_prefetch=1,
        grid=(1,),
        in_specs=[second, second, whole((rows, cols)), whole((rows, rows)), whole(meta.shape)],
        out_specs=tuple(whole(o) for o in outs),
    )
    return pl.pallas_call(
        pack_kernel,
        out_shape=tuple(jax.ShapeDtypeStruct(o, BF16) for o in outs),
        grid_spec=spec,
        compiler_params=params(),
        cost_estimate=cost(2 * rows * rows * cols, 3 << 20),
        name="pack",
    )(me, mine, core, across, pick, meta)


def attention_kernel(lmax, learners, me_ref, *refs):
    *kv_refs, q_ref, g_ref, out_ref, near_ref, far_ref, place_ref, slot_out = refs
    kv_refs = [kv_refs[0].at[me_ref[0] ^ i] for i in range(learners)]
    rows, cols = q_ref.shape
    lines = kv_refs[0].shape[0]
    block = rows // learners
    heads = cols // HEAD_DIM
    scale = 1.0 / HEAD_DIM**0.5
    meta = jnp.concatenate([ref[block:, :HEAD_DIM] for ref in kv_refs], axis=0)
    a, b = iota((rows, meta.shape[0]), 0), iota((rows, meta.shape[0]), 1)
    spread = (lax.div(a, block) * (lines - block) + lax.div(lax.rem(a, block), lmax) == b).astype(BF16)
    table = dot(spread, meta).astype(I32)
    inner = lax.rem(iota((rows, 1), 0), lmax)
    alive = inner < table[:, 0:1]
    target = jnp.where(alive, table[:, 1:2] * lmax + table[:, 2:3] + inner, -1)
    place_ref[...] = (iota((rows, rows), 1) == target).astype(BF16)
    size = HEAD_DIM
    a, b = iota((size, size), 0), iota((size, size), 1)
    near = (lax.div(a, lmax) == lax.div(b, lmax)) & (b <= a)
    for i in range(rows // size):
        span = slice(i * size, (i + 1) * size)
        first = i * size // block
        kv = jnp.concatenate([kv_refs[first + j][:block, :] for j in range(size // block)], axis=0)
        k, v = kv[:, :HEAD_DIM], kv[:, HEAD_DIM:]
        place = place_ref[span, :]
        q = dot(place, q_ref[...]).astype(BF16)
        g = dot(place, g_ref[...]).astype(BF16)
        q = jnp.concatenate([q[:, h * HEAD_DIM : (h + 1) * HEAD_DIM] for h in range(heads)], axis=0)
        g = jnp.concatenate([g[:, h * HEAD_DIM : (h + 1) * HEAD_DIM] for h in range(heads)], axis=0)
        allowed = jnp.tile(near & alive[span], (heads, 1))
        scores = jnp.where(allowed, dot(q, k, COLS_LAST) * scale, -1e30)
        top = jnp.max(scores, axis=1, keepdims=True)
        expo = jnp.exp(scores - top)
        total = jnp.sum(expo, axis=1, keepdims=True)
        probs = jnp.where(allowed, expo / total, 0.0)
        probs_b = probs.astype(BF16)
        out = dot(probs_b, v).astype(BF16)
        dprob = dot(g, v, COLS_LAST)
        delta = jnp.sum(g.astype(F32) * out.astype(F32), axis=1, keepdims=True)
        dscore_b = (probs * (dprob - delta)).astype(BF16)
        grad_ref, at = (near_ref, i * size) if i * size < rows // 2 else (far_ref, i * size - rows // 2)
        grad_ref[at : at + size, :HEAD_DIM] = (dot(dscore_b, q, ROWS_LAST) * scale).astype(BF16)
        grad_ref[at : at + size, HEAD_DIM:] = dot(probs_b, g, ROWS_LAST).astype(BF16)
        for h in range(heads):
            slot_out[span, h * HEAD_DIM : (h + 1) * HEAD_DIM] = out[h * size : (h + 1) * size]
    out_ref[...] = dot(place_ref[...], slot_out[...], ROWS_LAST).astype(BF16)


def attention(me, kvs, queries, out_grad, lmax, learners):
    rows, cols = queries.shape
    outs = ((rows, cols),) + ((rows // 2, 2 * HEAD_DIM),) * 2 + ((rows, rows),)
    spec = pltpu.PrefetchScalarGridSpec(
        num_scalar_prefetch=1,
        grid=(1,),
        in_specs=[whole(kv.shape) for kv in kvs] + [whole((rows, cols))] * 2,
        out_specs=tuple(whole(o) for o in outs),
        scratch_shapes=[pltpu.VMEM((rows, cols), BF16)],
    )
    return pl.pallas_call(
        functools.partial(attention_kernel, lmax, learners),
        out_shape=tuple(jax.ShapeDtypeStruct(o, BF16) for o in outs),
        grid_spec=spec,
        compiler_params=params(),
        cost_estimate=cost(8 * rows * rows * cols, 4 << 20),
        name="attention",
    )(me, *kvs, queries, out_grad)


def rows_kernel(me_ref, place_ref, *refs):
    *g_refs, wk_ref, wv_ref, out_ref, grads = refs

    @pl.when(pl.program_id(0) == 0)
    def _():
        half = grads.shape[1] // 2
        for i in range(4):
            g = jnp.concatenate([g_refs[2 * i][...], g_refs[2 * i + 1][...]], axis=0)
            part = dot(place_ref[...], g, ROWS_LAST).astype(BF16)
            at = pl.multiple_of((me_ref[0] ^ i) * HEAD_DIM, HEAD_DIM)
            grads[:, pl.ds(at, HEAD_DIM)] = part[:, :HEAD_DIM]
            grads[:, pl.ds(at + half, HEAD_DIM)] = part[:, HEAD_DIM:]

    half = grads.shape[1] // 2
    total = dot(grads[:, :half], wk_ref[...], COLS_LAST)
    out_ref[...] = (total + dot(grads[:, half:], wv_ref[...], COLS_LAST)).astype(BF16)


def row_grads(me, place, parts, w_key, w_value):
    feats, cols = w_key.shape
    rows = place.shape[0]
    step = 512
    spec = pltpu.PrefetchScalarGridSpec(
        num_scalar_prefetch=1,
        grid=(feats // step,),
        in_specs=[whole((rows, rows))]
        + [whole((rows // 2, 2 * HEAD_DIM))] * 8
        + [pl.BlockSpec((step, cols), lambda i, me: (i, 0))] * 2,
        out_specs=pl.BlockSpec((rows, step), lambda i, me: (0, i)),
        scratch_shapes=[pltpu.VMEM((rows, 2 * cols), BF16)],
    )
    return pl.pallas_call(
        rows_kernel,
        out_shape=jax.ShapeDtypeStruct((rows, feats), BF16),
        grid_spec=spec,
        compiler_params=params(),
        cost_estimate=cost(4 * rows * feats * cols, 8 << 20),
        name="row_grads",
    )(me, place, *parts, w_key, w_value)


def weights_kernel(x_refs, g_refs, out_refs):
    rows = x_refs[0].shape[1]
    group = len(x_refs) // 2
    block = rows // (2 * group)
    grads = []
    for f in range(group):
        g = [(g_refs[2 * (f ^ j) + b], j * block) for b in range(2) for j in range(group)]
        grads.append(jnp.concatenate([ref[at : at + block, :] for ref, at in g], axis=0))
    for side, out_ref in enumerate(out_refs):
        total = None
        for f, g in enumerate(grads):
            term = dot(x_refs[side * group + f][0], g, ROWS_LAST)
            total = term if total is None else total + term
        out_ref[...] = total.astype(out_ref.dtype)


def weight_grads(xs, pieces, half, dtype):
    _, rows, part = xs[0].shape
    out = (part, 2 * HEAD_DIM)

    def kernel(*refs):
        weights_kernel(refs[: len(xs)], refs[len(xs) : -2], refs[-2:])

    return pl.pallas_call(
        kernel,
        out_shape=(jax.ShapeDtypeStruct(out, dtype),) * 2,
        grid=(1,),
        in_specs=[pl.BlockSpec((1, rows, part), lambda i: (half, 0, 0))] * len(xs)
        + [whole(g.shape) for g in pieces],
        out_specs=(whole(out),) * 2,
        compiler_params=params(),
        cost_estimate=cost(4 * len(xs) * rows * part * HEAD_DIM, 6 << 20),
        name="weight_grads",
    )(*xs, *pieces)


def finish_kernel(learners, me_ref, *refs):
    *sums, k_ref, v_ref = refs
    for i in range(4):
        at = pl.ds(pl.multiple_of((me_ref[0] ^ i) * HEAD_DIM, HEAD_DIM), HEAD_DIM)
        total = (sums[2 * i][...] + sums[2 * i + 1][...].astype(F32)) / learners
        k_ref[:, at] = total[:, :HEAD_DIM]
        v_ref[:, at] = total[:, HEAD_DIM:]


def finish(me, sums, learners):
    part, cols = sums[0].shape
    out = (part, 2 * cols)
    spec = pltpu.PrefetchScalarGridSpec(
        num_scalar_prefetch=1,
        grid=(1,),
        in_specs=[whole((part, cols))] * 8,
        out_specs=(whole(out),) * 2,
    )
    return pl.pallas_call(
        functools.partial(finish_kernel, float(learners)),
        out_shape=(jax.ShapeDtypeStruct(out, F32),) * 2,
        grid_spec=spec,
        compiler_params=params(),
        cost_estimate=cost(part * cols, 2 << 20),
        name="finish",
    )(me, *sums)


def swap(x, axis, code):
    size = lax.axis_size(axis)
    return lax.ppermute(x, axis, [(i, i ^ code) for i in range(size)])


def after(x, *earlier):
    return lax.optimization_barrier((x,) + earlier)[0]


def local(roll_x, lengths, dest, offsets, queries, out_grad, w_key, w_value):
    learners, heads = lax.axis_size("dp"), lax.axis_size("mp")
    samp, lmax, feats = roll_x.shape
    per = (samp + learners - 1) // learners
    x = roll_x.reshape(samp * lmax, feats)
    m = lax.axis_index("mp").astype(I32).reshape(1)
    d = lax.axis_index("dp").astype(I32).reshape(1)

    away, mine = project(m, x, w_key, w_value)
    core = swap(away, "mp", 1)
    half = mine[1] + core[1]
    across = swap(half, "mp", 2)
    *xs, pick, meta = slots(d, dest, lengths, offsets, after(x, half), learners, per)
    xs = [xs[0]] + [swap(xs[f], "dp", f) for f in range(1, learners // 2)]
    kv = pack(d, mine, core, across, pick, meta)
    kv = lax.all_to_all(kv[0], "dp", split_axis=0, concat_axis=0, tiled=True)

    attn_out, grads, beyond, place = attention(d, [kv], queries, out_grad, lmax, learners)

    xs = xs + [swap(b, "mp", 1) for b in xs]
    there = swap(beyond, "dp", 4)
    near = {(0, 0, 0): grads, (0, 0, 1): there}
    hops = [
        ((0, 0), "dp", 1), ((0, 0), "dp", 2), ((0, 0), "mp", 2), ((2, 0), "dp", 1),
        ((1, 0), "mp", 2), ((0, 1), "dp", 2), ((1, 1), "dp", 2),
    ]
    for part in range(2):
        for (code, far), axis, step in hops:
            key = (code ^ step, far, part) if axis == "dp" else (code, 1 - far, part)
            near[key] = swap(near[code, far, part], axis, step)
    across = swap(beyond, "mp", 2)
    own = [grads, beyond, swap(grads, "mp", 1), swap(beyond, "mp", 1)]
    own += [near[0, 1, 0], across, swap(near[0, 1, 0], "mp", 1), swap(across, "mp", 1)]
    sums = [None] * 8
    for far in range(2):
        pieces = [near[c, far, b] for c in range(learners // 2) for b in range(2)]
        send = weight_grads(xs, pieces, 1, BF16)
        sums[4 * far + 1] = swap(send[0], "dp", 4)
        sums[4 * far + 3] = swap(send[1], ("dp", "mp"), 4 * heads + 1)
        sums[4 * far], keep = weight_grads(xs, pieces, 0, F32)
        sums[4 * far + 2] = swap(keep, "mp", 1)
    grad_x = row_grads(m, place, own, w_key, w_value)
    grad_wk, grad_wv = finish(m, sums, learners)
    return (attn_out, grad_x, grad_wk, grad_wv)


def solution(mesh):
    dp, mp = mesh.shape["dp"], mesh.shape["mp"]
    body = local if dp == 8 and mp == 4 else general
    return jax.shard_map(
        body,
        mesh=mesh,
        in_specs=(
            P("dp", None, "mp"),
            P("dp"),
            P("dp"),
            P("dp"),
            P("dp", "mp"),
            P("dp", "mp"),
            P("mp", None),
            P("mp", None),
        ),
        out_specs=(P("dp", "mp"), P("dp", "mp"), P(("mp", "dp"), None), P(("mp", "dp"), None)),
        check_vma=False,
    )
```

```python
import functools

import jax
import jax.numpy as jnp
from jax import lax
from jax.experimental import pallas as pl
from jax.experimental.pallas import tpu as pltpu
from jax.sharding import PartitionSpec as P

HEAD_DIM = 128


def attend(qs, ks, vs, grads, mask):
    scale = 1.0 / qs.shape[-1] ** 0.5
    scores = jnp.einsum("bqkge,bmke->bkgqm", qs, ks, preferred_element_type=jnp.float32) * scale
    allowed = mask[:, None, None, :, :]
    scores = jnp.where(allowed, scores, -1e30)
    top = jnp.max(scores, axis=-1, keepdims=True)
    expo = jnp.exp(scores - top)
    total = jnp.sum(expo, axis=-1, keepdims=True)
    probs = jnp.where(allowed, expo / total, 0.0)
    probs_b = probs.astype(jnp.bfloat16)
    out = jnp.einsum("bkgqm,bmke->bqkge", probs_b, vs, preferred_element_type=jnp.float32).astype(
        jnp.bfloat16
    )
    dprob = jnp.einsum("bqkge,bmke->bkgqm", grads, vs, preferred_element_type=jnp.float32)
    delta = jnp.einsum("bqkge,bqkge->bkgq", grads, out, preferred_element_type=jnp.float32)
    dscore = probs * (dprob - delta[..., None])
    dscore_b = dscore.astype(jnp.bfloat16)
    key_grad = (
        jnp.einsum("bkgqm,bqkge->bmke", dscore_b, qs, preferred_element_type=jnp.float32) * scale
    ).astype(jnp.bfloat16)
    val_grad = jnp.einsum(
        "bkgqm,bqkge->bmke", probs_b, grads, preferred_element_type=jnp.float32
    ).astype(jnp.bfloat16)
    return (out, key_grad, val_grad)


def input_grads(key_all, val_all, w_key, w_value):
    contract = (((1,), (1,)), ((), ()))
    total = lax.dot_general(key_all, w_key, contract, preferred_element_type=jnp.float32)
    total = total + lax.dot_general(val_all, w_value, contract, preferred_element_type=jnp.float32)
    return total.astype(jnp.bfloat16)


def general(roll_x, lengths, dest, offsets, queries, out_grad, w_key, w_value):
    learners = lax.axis_size("dp")
    samp, lmax, feats = roll_x.shape
    rows = queries.shape[0]
    slots_per = (samp + learners - 1) // learners
    slot_count = learners * slots_per
    order = jnp.arange(samp, dtype=jnp.int32)
    earlier = (dest[None, :] == dest[:, None]) & (order[None, :] < order[:, None])
    rank = jnp.sum(earlier.astype(jnp.int32), axis=1)
    slot = dest * slots_per + rank
    match = slot[None, :] == jnp.arange(slot_count, dtype=jnp.int32)[:, None]
    filled = jnp.any(match, axis=1)
    pick = jnp.sum(jnp.where(match, order[None, :], 0), axis=1)
    send_x = jnp.where(
        filled[:, None, None], jnp.take(roll_x, pick, axis=0), jnp.zeros((), jnp.bfloat16)
    )
    send_len = jnp.where(filled, jnp.take(lengths, pick), 0)
    send_off = jnp.where(filled, jnp.take(offsets, pick), 0)
    recv_x, recv_len, recv_off = (
        lax.all_to_all(send_x, "dp", split_axis=0, concat_axis=0, tiled=True),
        lax.all_to_all(send_len, "dp", split_axis=0, concat_axis=0, tiled=True),
        lax.all_to_all(send_off, "dp", split_axis=0, concat_axis=0, tiled=True),
    )
    position = jnp.arange(lmax, dtype=jnp.int32)
    live = position[None, :] < recv_len[:, None]
    target = jnp.where(live, recv_off[:, None] + position[None, :], rows).astype(jnp.int32)
    flat = target.reshape(-1)
    packed = (
        jnp.zeros((rows, feats), jnp.bfloat16).at[flat].set(recv_x.reshape(-1, feats), mode="drop")
    )
    part_k = jnp.dot(packed, w_key, preferred_element_type=jnp.float32)
    part_v = jnp.dot(packed, w_value, preferred_element_type=jnp.float32)
    key_mine, val_mine = (
        lax.psum_scatter(part_k, "mp", scatter_dimension=1, tiled=True),
        lax.psum_scatter(part_v, "mp", scatter_dimension=1, tiled=True),
    )
    keys = key_mine.astype(jnp.bfloat16)
    vals = val_mine.astype(jnp.bfloat16)
    local_heads = keys.shape[1] // HEAD_DIM
    q_cols = queries.shape[1]
    group = q_cols // (local_heads * HEAD_DIM)
    slot_ids = jnp.broadcast_to(
        jnp.arange(slot_count, dtype=jnp.int32)[:, None], (slot_count, lmax)
    )
    seg = jnp.full((rows,), -1, jnp.int32).at[flat].set(slot_ids.reshape(-1), mode="drop")
    rowpos = jnp.arange(rows, dtype=jnp.int32)
    mask = (
        (seg[:, None] == seg[None, :]) & (seg[:, None] >= 0) & (rowpos[None, :] <= rowpos[:, None])
    )
    out, key_grad, val_grad = attend(
        queries.reshape(1, rows, local_heads, group, HEAD_DIM),
        keys.reshape(1, rows, local_heads, HEAD_DIM),
        vals.reshape(1, rows, local_heads, HEAD_DIM),
        out_grad.reshape(1, rows, local_heads, group, HEAD_DIM),
        mask[None],
    )
    attn_out = out.reshape(rows, q_cols)
    key_grad = key_grad.reshape(rows, local_heads * HEAD_DIM)
    val_grad = val_grad.reshape(rows, local_heads * HEAD_DIM)
    key_all, val_all = (
        lax.all_gather(key_grad, "mp", axis=1, tiled=True),
        lax.all_gather(val_grad, "mp", axis=1, tiled=True),
    )
    grad_x = input_grads(key_all, val_all, w_key, w_value)
    contract = (((0,), (0,)), ((), ()))
    whole_k = lax.dot_general(packed, key_all, contract, preferred_element_type=jnp.float32)
    whole_v = lax.dot_general(packed, val_all, contract, preferred_element_type=jnp.float32)
    sum_k, sum_v = (
        lax.psum_scatter(whole_k, "dp", scatter_dimension=0, tiled=True),
        lax.psum_scatter(whole_v, "dp", scatter_dimension=0, tiled=True),
    )
    return (attn_out, grad_x, sum_k / learners, sum_v / learners)


BF16, F32, I32 = jnp.bfloat16, jnp.float32, jnp.int32
ROWS_LAST = (((0,), (0,)), ((), ()))
COLS_LAST = (((1,), (1,)), ((), ()))


def dot(a, b, dims=(((1,), (0,)), ((), ()))):
    return lax.dot_general(a, b, dims, preferred_element_type=F32)


def iota(shape, dim):
    return lax.broadcasted_iota(I32, shape, dim)


def params(mib=44):
    return pltpu.CompilerParams(
        dimension_semantics=("arbitrary",), vmem_limit_bytes=mib * 1024 * 1024
    )


def cost(flops, moved):
    return pl.CostEstimate(flops=0, bytes_accessed=0, transcendentals=0)


def whole(shape):
    zeros = (0,) * len(shape)
    return pl.BlockSpec(shape, lambda *_: zeros)


def project_kernel(me_ref, x_ref, wk_ref, wv_ref, away_ref, keep_ref):
    other = pl.multiple_of((lax.rem(me_ref[0], 2) ^ 1) * HEAD_DIM, HEAD_DIM)
    for at, ref in ((other, away_ref), (HEAD_DIM - other, keep_ref)):
        span = pl.ds(pl.multiple_of(at, HEAD_DIM), HEAD_DIM)
        ref[...] = dot(x_ref[...], jnp.concatenate([wk_ref[:, span], wv_ref[:, span]], axis=1))


def project(me, x, w_key, w_value, far):
    rows, feats = x.shape
    step = rows // 2
    out = (rows, 2 * HEAD_DIM)
    weights = pl.BlockSpec((feats, 2 * HEAD_DIM), lambda i, me: (0, lax.div(me[0], 2) ^ far))
    block = pl.BlockSpec((step, 2 * HEAD_DIM), lambda i, me: (i, 0))
    spec = pltpu.PrefetchScalarGridSpec(
        num_scalar_prefetch=1,
        grid=(rows // step,),
        in_specs=[pl.BlockSpec((step, feats), lambda i, me: (i, 0)), weights, weights],
        out_specs=(block, block),
    )
    return pl.pallas_call(
        project_kernel,
        out_shape=(jax.ShapeDtypeStruct(out, F32),) * 2,
        grid_spec=spec,
        compiler_params=params(58),
        cost_estimate=cost(8 * rows * feats * HEAD_DIM, 5 << 20),
        name="project",
    )(me, x, w_key, w_value)


def slots_kernel(per, me_ref, dest_ref, len_ref, off_ref, x_ref, *refs):
    *xs_refs, pick_ref, meta_ref = refs
    samp = dest_ref.shape[1]
    rows, feats = x_ref.shape
    lmax = rows // samp
    row = dest_ref[...]
    a, b = iota((samp, samp), 0), iota((samp, samp), 1)
    col = jnp.sum(jnp.where(a == b, row, 0), axis=1, keepdims=True)
    rank = jnp.sum(jnp.where((col == row) & (a < b), 1, 0), axis=0, keepdims=True)
    slot = (row ^ me_ref[0]) * per + rank
    a, b = iota((samp, rows), 0), iota((samp, rows), 1)
    spread = (a == lax.div(b, lmax)).astype(BF16)
    wide = dot(jnp.broadcast_to(slot, (8, samp)).astype(BF16), spread)[0:1]
    source = wide.astype(I32) * lmax + lax.rem(iota((1, rows), 1), lmax)
    pick_ref[...] = (iota((rows, rows), 0) == source).astype(BF16)
    held = iota((samp, samp), 0) == slot
    size = jnp.sum(jnp.where(held, len_ref[...], 0), axis=1, keepdims=True)
    start = jnp.sum(jnp.where(held, off_ref[...], 0), axis=1, keepdims=True)
    lane = iota((samp, meta_ref.shape[2]), 1)
    table = jnp.where(lane == 0, size, jnp.where(lane == 2, lax.rem(start, lmax), 0))
    table = jnp.where(lane == 1, lax.div(start, lmax), table).astype(BF16)
    lines = meta_ref.shape[0] * meta_ref.shape[1]
    a, b = iota((lines, samp), 0), iota((lines, samp), 1)
    place = (b == lax.div(a, 16) * per + lax.rem(a, 16)) & (lax.rem(a, 16) < per)
    meta_ref[...] = dot(place.astype(BF16), table).astype(BF16).reshape(meta_ref.shape)
    part = xs_refs[0].shape[2]
    for f, ref in enumerate(xs_refs):
        for h in range(2):
            at = pl.multiple_of((me_ref[0] ^ (f + h * len(xs_refs))) * part, part)
            ref[h] = dot(pick_ref[...], x_ref[:, pl.ds(at, part)]).astype(BF16)


def slots(me, dest, lengths, offsets, x, learners, per):
    rows, feats = x.shape
    samp = dest.shape[0]
    part = feats // learners
    line = whole((1, samp))
    xs = ((2, rows, part),) * (learners // 2)
    outs = xs + ((rows, rows), (learners, 16, 2 * HEAD_DIM))
    spec = pltpu.PrefetchScalarGridSpec(
        num_scalar_prefetch=1,
        grid=(1,),
        in_specs=[line, line, line, whole((rows, feats))],
        out_specs=tuple(whole(o) for o in outs),
    )
    return pl.pallas_call(
        functools.partial(slots_kernel, per),
        out_shape=tuple(jax.ShapeDtypeStruct(o, BF16) for o in outs),
        grid_spec=spec,
        compiler_params=params(),
        cost_estimate=cost(2 * rows * rows * feats, 5 << 20),
        name="slots",
    )(me, dest.reshape(1, samp), lengths.reshape(1, samp), offsets.reshape(1, samp), x)


def pack_kernel(me_ref, mine_ref, core_ref, across_ref, pick_ref, meta_ref, *out_refs):
    total = (mine_ref[...] + core_ref[...]) + across_ref[...]
    placed = dot(pick_ref[...], total.astype(BF16)).astype(BF16)
    learners = meta_ref.shape[0]
    block = placed.shape[0] // learners
    for i in range(learners):
        ref = out_refs[0].at[me_ref[0] ^ i]
        ref[:block, :] = placed[i * block : (i + 1) * block]
        ref[block:, :] = meta_ref[i]


def pack(me, mine, core, across, pick, meta):
    rows, cols = across.shape
    learners, extra, _ = meta.shape
    out = (rows // learners + extra, cols)
    outs = ((learners,) + out,)
    part = whole((rows, cols))
    spec = pltpu.PrefetchScalarGridSpec(
        num_scalar_prefetch=1,
        grid=(1,),
        in_specs=[part, part, part, whole((rows, rows)), whole(meta.shape)],
        out_specs=tuple(whole(o) for o in outs),
    )
    return pl.pallas_call(
        pack_kernel,
        out_shape=tuple(jax.ShapeDtypeStruct(o, BF16) for o in outs),
        grid_spec=spec,
        compiler_params=params(),
        cost_estimate=cost(2 * rows * rows * cols, 3 << 20),
        name="pack",
    )(me, mine, core, across, pick, meta)


def attention_kernel(lmax, learners, half, me_ref, kv_ref, q_ref, g_ref, grad_ref, out_ref, place_ref):
    rows, cols = q_ref.shape
    block = rows // learners
    heads = cols // HEAD_DIM
    scale = 1.0 / HEAD_DIM**0.5
    count = learners // 2
    kv_refs = [kv_ref.at[me_ref[0] ^ (half * count + i)] for i in range(count)]
    lines = kv_ref.shape[1]
    meta = jnp.concatenate([ref[block:, :HEAD_DIM] for ref in kv_refs], axis=0)
    a, b = iota((rows // 2, meta.shape[0]), 0), iota((rows // 2, meta.shape[0]), 1)
    spread = (lax.div(a, block) * (lines - block) + lax.div(lax.rem(a, block), lmax) == b).astype(BF16)
    table = dot(spread, meta).astype(I32)
    inner = lax.rem(iota((rows // 2, 1), 0), lmax)
    alive = inner < table[:, 0:1]
    target = jnp.where(alive, table[:, 1:2] * lmax + table[:, 2:3] + inner, -1)
    place_ref[...] = (iota((rows // 2, rows), 1) == target).astype(BF16)
    size = HEAD_DIM
    a, b = iota((size, size), 0), iota((size, size), 1)
    near = (lax.div(a, lmax) == lax.div(b, lmax)) & (b <= a)
    for i in range(rows // 2 // size):
        span = slice(i * size, (i + 1) * size)
        first = i * size // block
        kv = jnp.concatenate([kv_refs[first + j][:block, :] for j in range(size // block)], axis=0)
        k, v = kv[:, :HEAD_DIM], kv[:, HEAD_DIM:]
        place = place_ref[span, :]
        q = dot(place, q_ref[...]).astype(BF16)
        g = dot(place, g_ref[...]).astype(BF16)
        q = jnp.concatenate([q[:, h * HEAD_DIM : (h + 1) * HEAD_DIM] for h in range(heads)], axis=0)
        g = jnp.concatenate([g[:, h * HEAD_DIM : (h + 1) * HEAD_DIM] for h in range(heads)], axis=0)
        allowed = jnp.tile(near & alive[span], (heads, 1))
        scores = jnp.where(allowed, dot(q, k, COLS_LAST) * scale, -1e30)
        top = jnp.max(scores, axis=1, keepdims=True)
        expo = jnp.exp(scores - top)
        total = jnp.sum(expo, axis=1, keepdims=True)
        probs = jnp.where(allowed, expo / total, 0.0)
        probs_b = probs.astype(BF16)
        out = dot(probs_b, v).astype(BF16)
        dprob = dot(g, v, COLS_LAST)
        delta = jnp.sum(g.astype(F32) * out.astype(F32), axis=1, keepdims=True)
        dscore_b = (probs * (dprob - delta)).astype(BF16)
        grad_ref[span, :HEAD_DIM] = (dot(dscore_b, q, ROWS_LAST) * scale).astype(BF16)
        grad_ref[span, HEAD_DIM:] = dot(probs_b, g, ROWS_LAST).astype(BF16)
        for h in range(heads):
            out_ref[span, h * HEAD_DIM : (h + 1) * HEAD_DIM] = out[h * size : (h + 1) * size]


def attention(me, kv, queries, out_grad, lmax, learners, half):
    rows, cols = queries.shape
    outs = ((rows // 2, 2 * HEAD_DIM), (rows // 2, cols), (rows // 2, rows))
    spec = pltpu.PrefetchScalarGridSpec(
        num_scalar_prefetch=1,
        grid=(1,),
        in_specs=[whole(kv.shape)] + [whole((rows, cols))] * 2,
        out_specs=tuple(whole(o) for o in outs),
    )
    return pl.pallas_call(
        functools.partial(attention_kernel, lmax, learners, half),
        out_shape=tuple(jax.ShapeDtypeStruct(o, BF16) for o in outs),
        grid_spec=spec,
        compiler_params=params(),
        cost_estimate=cost(4 * rows * rows * cols, 4 << 20),
        name="attention",
    )(me, kv, queries, out_grad)


def packed_rows_kernel(place0, place1, out0, out1, out_ref):
    total = dot(place0[...], out0[...], ROWS_LAST) + dot(place1[...], out1[...], ROWS_LAST)
    out_ref[...] = total.astype(BF16)


def packed_rows(place, outs):
    half, cols = outs[0].shape
    rows = place[0].shape[1]
    return pl.pallas_call(
        packed_rows_kernel,
        out_shape=jax.ShapeDtypeStruct((rows, cols), BF16),
        grid=(1,),
        in_specs=[whole((half, rows))] * 2 + [whole((half, cols))] * 2,
        out_specs=whole((rows, cols)),
        compiler_params=params(),
        cost_estimate=cost(4 * half * rows * cols, 3 << 20),
        name="packed_rows",
    )(*place, *outs)


def rows_kernel(me_ref, place0, place1, *refs):
    *g_refs, wk_ref, wv_ref, out_ref, grads = refs

    @pl.when(pl.program_id(0) == 0)
    def _():
        half = grads.shape[1] // 2
        for i in range(4):
            part = dot(place0[...], g_refs[2 * i][...], ROWS_LAST)
            part = (part + dot(place1[...], g_refs[2 * i + 1][...], ROWS_LAST)).astype(BF16)
            at = pl.multiple_of((me_ref[0] ^ i) * HEAD_DIM, HEAD_DIM)
            grads[:, pl.ds(at, HEAD_DIM)] = part[:, :HEAD_DIM]
            grads[:, pl.ds(at + half, HEAD_DIM)] = part[:, HEAD_DIM:]

    half = grads.shape[1] // 2
    total = dot(grads[:, :half], wk_ref[...], COLS_LAST)
    out_ref[...] = (total + dot(grads[:, half:], wv_ref[...], COLS_LAST)).astype(BF16)


def row_grads(me, place, parts, w_key, w_value):
    feats, cols = w_key.shape
    rows = place[0].shape[1]
    step = 512
    spec = pltpu.PrefetchScalarGridSpec(
        num_scalar_prefetch=1,
        grid=(feats // step,),
        in_specs=[whole((rows // 2, rows))] * 2
        + [whole((rows // 2, 2 * HEAD_DIM))] * 8
        + [pl.BlockSpec((step, cols), lambda i, me: (i, 0))] * 2,
        out_specs=pl.BlockSpec((rows, step), lambda i, me: (0, i)),
        scratch_shapes=[pltpu.VMEM((rows, 2 * cols), BF16)],
    )
    return pl.pallas_call(
        rows_kernel,
        out_shape=jax.ShapeDtypeStruct((rows, feats), BF16),
        grid_spec=spec,
        compiler_params=params(),
        cost_estimate=cost(4 * rows * feats * cols, 8 << 20),
        name="row_grads",
    )(me, *place, *parts, w_key, w_value)


def weights_kernel(x_refs, g_refs, out_refs):
    rows = x_refs[0].shape[1]
    group = len(x_refs) // 2
    block = rows // (2 * group)
    grads = []
    for f in range(group):
        g = [(g_refs[2 * (f ^ j) + b], j * block) for b in range(2) for j in range(group)]
        grads.append(jnp.concatenate([ref[at : at + block, :] for ref, at in g], axis=0))
    for side, out_ref in enumerate(out_refs):
        total = None
        for f, g in enumerate(grads):
            term = dot(x_refs[side * group + f][0], g, ROWS_LAST)
            total = term if total is None else total + term
        out_ref[...] = total.astype(out_ref.dtype)


def weight_grads(xs, pieces, half, dtype):
    _, rows, part = xs[0].shape
    out = (part, 2 * HEAD_DIM)

    def kernel(*refs):
        weights_kernel(refs[: len(xs)], refs[len(xs) : -2], refs[-2:])

    return pl.pallas_call(
        kernel,
        out_shape=(jax.ShapeDtypeStruct(out, dtype),) * 2,
        grid=(1,),
        in_specs=[pl.BlockSpec((1, rows, part), lambda i: (half, 0, 0))] * len(xs)
        + [whole(g.shape) for g in pieces],
        out_specs=(whole(out),) * 2,
        compiler_params=params(),
        cost_estimate=cost(4 * len(xs) * rows * part * HEAD_DIM, 6 << 20),
        name="weight_grads",
    )(*xs, *pieces)


def finish_kernel(learners, me_ref, *refs):
    *sums, k_ref, v_ref = refs
    for i in range(4):
        at = pl.ds(pl.multiple_of((me_ref[0] ^ i) * HEAD_DIM, HEAD_DIM), HEAD_DIM)
        total = (sums[2 * i][...] + sums[2 * i + 1][...].astype(F32)) / learners
        k_ref[:, at] = total[:, :HEAD_DIM]
        v_ref[:, at] = total[:, HEAD_DIM:]


def finish(me, sums, learners):
    part, cols = sums[0].shape
    out = (part, 2 * cols)
    spec = pltpu.PrefetchScalarGridSpec(
        num_scalar_prefetch=1,
        grid=(1,),
        in_specs=[whole((part, cols))] * 8,
        out_specs=(whole(out),) * 2,
    )
    return pl.pallas_call(
        functools.partial(finish_kernel, float(learners)),
        out_shape=(jax.ShapeDtypeStruct(out, F32),) * 2,
        grid_spec=spec,
        compiler_params=params(),
        cost_estimate=cost(part * cols, 2 << 20),
        name="finish",
    )(me, *sums)


def swap(x, axis, code):
    size = lax.axis_size(axis)
    return lax.ppermute(x, axis, [(i, i ^ code) for i in range(size)])


def after(x, *earlier):
    return lax.optimization_barrier((x,) + earlier)[0]


def local(roll_x, lengths, dest, offsets, queries, out_grad, w_key, w_value):
    learners, heads = lax.axis_size("dp"), lax.axis_size("mp")
    samp, lmax, feats = roll_x.shape
    per = (samp + learners - 1) // learners
    x = roll_x.reshape(samp * lmax, feats)
    m = lax.axis_index("mp").astype(I32).reshape(1)
    d = lax.axis_index("dp").astype(I32).reshape(1)

    away, keep = project(m, x, w_key, w_value, 1)
    core = swap(away, "mp", 1)
    *xs, pick, meta = slots(d, dest, lengths, offsets, after(x, away), learners, per)
    half = after(keep, pick) + core
    xs = [xs[0]] + [swap(after(xs[f], half), "dp", f) for f in range(1, learners // 2)]
    across = swap(half, "mp", 2)
    away, keep = project(m, after(x, half), w_key, w_value, 0)
    core = swap(away, "mp", 1)
    kv = pack(d, keep, core, across, pick, meta)
    kv = lax.all_to_all(kv[0], "dp", split_axis=0, concat_axis=0, tiled=True)

    beyond, out1, place1 = attention(d, kv, queries, out_grad, lmax, learners, 1)
    there = swap(beyond, "dp", 4)
    grads, out0, place0 = attention(d, after(kv, beyond), queries, out_grad, lmax, learners, 0)
    place = [place0, place1]

    xs = xs + [swap(b, "mp", 1) for b in xs]
    near = {(0, 0, 0): grads, (0, 0, 1): there}
    hops = [
        ((0, 0), "dp", 1), ((0, 0), "dp", 2), ((0, 0), "mp", 2), ((2, 0), "dp", 1),
        ((1, 0), "mp", 2), ((0, 1), "dp", 2), ((1, 1), "dp", 2),
    ]
    for part in range(2):
        for (code, far), axis, step in hops:
            key = (code ^ step, far, part) if axis == "dp" else (code, 1 - far, part)
            near[key] = swap(near[code, far, part], axis, step)
    across = swap(beyond, "mp", 2)
    own = [grads, beyond, swap(grads, "mp", 1), swap(beyond, "mp", 1)]
    own += [near[0, 1, 0], across, swap(near[0, 1, 0], "mp", 1), swap(across, "mp", 1)]
    sums = [None] * 8
    for far in range(2):
        pieces = [near[c, far, b] for c in range(learners // 2) for b in range(2)]
        send = weight_grads(xs, pieces, 1, BF16)
        sums[4 * far + 1] = swap(send[0], "dp", 4)
        sums[4 * far + 3] = swap(send[1], ("dp", "mp"), 4 * heads + 1)
        sums[4 * far], keep = weight_grads(xs, pieces, 0, F32)
        sums[4 * far + 2] = swap(keep, "mp", 1)
    attn_out = packed_rows(place, [out0, out1])
    grad_x = row_grads(m, place, own, w_key, w_value)
    grad_wk, grad_wv = finish(m, sums, learners)
    return (attn_out, grad_x, grad_wk, grad_wv)


def solution(mesh):
    dp, mp = mesh.shape["dp"], mesh.shape["mp"]
    body = local if dp == 8 and mp == 4 else general
    return jax.shard_map(
        body,
        mesh=mesh,
        in_specs=(
            P("dp", None, "mp"),
            P("dp"),
            P("dp"),
            P("dp"),
            P("dp", "mp"),
            P("dp", "mp"),
            P("mp", None),
            P("mp", None),
        ),
        out_specs=(P("dp", "mp"), P("dp", "mp"), P(("mp", "dp"), None), P(("mp", "dp"), None)),
        check_vma=False,
    )
```

```python
import functools

import jax
import jax.numpy as jnp
from jax import lax
from jax.experimental import pallas as pl
from jax.experimental.pallas import tpu as pltpu
from jax.sharding import PartitionSpec as P

HEAD_DIM = 128


def attend(qs, ks, vs, grads, mask):
    scale = 1.0 / qs.shape[-1] ** 0.5
    scores = jnp.einsum("bqkge,bmke->bkgqm", qs, ks, preferred_element_type=jnp.float32) * scale
    allowed = mask[:, None, None, :, :]
    scores = jnp.where(allowed, scores, -1e30)
    top = jnp.max(scores, axis=-1, keepdims=True)
    expo = jnp.exp(scores - top)
    total = jnp.sum(expo, axis=-1, keepdims=True)
    probs = jnp.where(allowed, expo / total, 0.0)
    probs_b = probs.astype(jnp.bfloat16)
    out = jnp.einsum("bkgqm,bmke->bqkge", probs_b, vs, preferred_element_type=jnp.float32).astype(
        jnp.bfloat16
    )
    dprob = jnp.einsum("bqkge,bmke->bkgqm", grads, vs, preferred_element_type=jnp.float32)
    delta = jnp.einsum("bqkge,bqkge->bkgq", grads, out, preferred_element_type=jnp.float32)
    dscore = probs * (dprob - delta[..., None])
    dscore_b = dscore.astype(jnp.bfloat16)
    key_grad = (
        jnp.einsum("bkgqm,bqkge->bmke", dscore_b, qs, preferred_element_type=jnp.float32) * scale
    ).astype(jnp.bfloat16)
    val_grad = jnp.einsum(
        "bkgqm,bqkge->bmke", probs_b, grads, preferred_element_type=jnp.float32
    ).astype(jnp.bfloat16)
    return (out, key_grad, val_grad)


def input_grads(key_all, val_all, w_key, w_value):
    contract = (((1,), (1,)), ((), ()))
    total = lax.dot_general(key_all, w_key, contract, preferred_element_type=jnp.float32)
    total = total + lax.dot_general(val_all, w_value, contract, preferred_element_type=jnp.float32)
    return total.astype(jnp.bfloat16)


def general(roll_x, lengths, dest, offsets, queries, out_grad, w_key, w_value):
    learners = lax.axis_size("dp")
    samp, lmax, feats = roll_x.shape
    rows = queries.shape[0]
    slots_per = (samp + learners - 1) // learners
    slot_count = learners * slots_per
    order = jnp.arange(samp, dtype=jnp.int32)
    earlier = (dest[None, :] == dest[:, None]) & (order[None, :] < order[:, None])
    rank = jnp.sum(earlier.astype(jnp.int32), axis=1)
    slot = dest * slots_per + rank
    match = slot[None, :] == jnp.arange(slot_count, dtype=jnp.int32)[:, None]
    filled = jnp.any(match, axis=1)
    pick = jnp.sum(jnp.where(match, order[None, :], 0), axis=1)
    send_x = jnp.where(
        filled[:, None, None], jnp.take(roll_x, pick, axis=0), jnp.zeros((), jnp.bfloat16)
    )
    send_len = jnp.where(filled, jnp.take(lengths, pick), 0)
    send_off = jnp.where(filled, jnp.take(offsets, pick), 0)
    recv_x, recv_len, recv_off = (
        lax.all_to_all(send_x, "dp", split_axis=0, concat_axis=0, tiled=True),
        lax.all_to_all(send_len, "dp", split_axis=0, concat_axis=0, tiled=True),
        lax.all_to_all(send_off, "dp", split_axis=0, concat_axis=0, tiled=True),
    )
    position = jnp.arange(lmax, dtype=jnp.int32)
    live = position[None, :] < recv_len[:, None]
    target = jnp.where(live, recv_off[:, None] + position[None, :], rows).astype(jnp.int32)
    flat = target.reshape(-1)
    packed = (
        jnp.zeros((rows, feats), jnp.bfloat16).at[flat].set(recv_x.reshape(-1, feats), mode="drop")
    )
    part_k = jnp.dot(packed, w_key, preferred_element_type=jnp.float32)
    part_v = jnp.dot(packed, w_value, preferred_element_type=jnp.float32)
    key_mine, val_mine = (
        lax.psum_scatter(part_k, "mp", scatter_dimension=1, tiled=True),
        lax.psum_scatter(part_v, "mp", scatter_dimension=1, tiled=True),
    )
    keys = key_mine.astype(jnp.bfloat16)
    vals = val_mine.astype(jnp.bfloat16)
    local_heads = keys.shape[1] // HEAD_DIM
    q_cols = queries.shape[1]
    group = q_cols // (local_heads * HEAD_DIM)
    slot_ids = jnp.broadcast_to(
        jnp.arange(slot_count, dtype=jnp.int32)[:, None], (slot_count, lmax)
    )
    seg = jnp.full((rows,), -1, jnp.int32).at[flat].set(slot_ids.reshape(-1), mode="drop")
    rowpos = jnp.arange(rows, dtype=jnp.int32)
    mask = (
        (seg[:, None] == seg[None, :]) & (seg[:, None] >= 0) & (rowpos[None, :] <= rowpos[:, None])
    )
    out, key_grad, val_grad = attend(
        queries.reshape(1, rows, local_heads, group, HEAD_DIM),
        keys.reshape(1, rows, local_heads, HEAD_DIM),
        vals.reshape(1, rows, local_heads, HEAD_DIM),
        out_grad.reshape(1, rows, local_heads, group, HEAD_DIM),
        mask[None],
    )
    attn_out = out.reshape(rows, q_cols)
    key_grad = key_grad.reshape(rows, local_heads * HEAD_DIM)
    val_grad = val_grad.reshape(rows, local_heads * HEAD_DIM)
    key_all, val_all = (
        lax.all_gather(key_grad, "mp", axis=1, tiled=True),
        lax.all_gather(val_grad, "mp", axis=1, tiled=True),
    )
    grad_x = input_grads(key_all, val_all, w_key, w_value)
    contract = (((0,), (0,)), ((), ()))
    whole_k = lax.dot_general(packed, key_all, contract, preferred_element_type=jnp.float32)
    whole_v = lax.dot_general(packed, val_all, contract, preferred_element_type=jnp.float32)
    sum_k, sum_v = (
        lax.psum_scatter(whole_k, "dp", scatter_dimension=0, tiled=True),
        lax.psum_scatter(whole_v, "dp", scatter_dimension=0, tiled=True),
    )
    return (attn_out, grad_x, sum_k / learners, sum_v / learners)


BF16, F32, I32 = jnp.bfloat16, jnp.float32, jnp.int32
ROWS_LAST = (((0,), (0,)), ((), ()))
COLS_LAST = (((1,), (1,)), ((), ()))


def dot(a, b, dims=(((1,), (0,)), ((), ()))):
    return lax.dot_general(a, b, dims, preferred_element_type=F32)


def iota(shape, dim):
    return lax.broadcasted_iota(I32, shape, dim)


def params(mib=44):
    return pltpu.CompilerParams(
        dimension_semantics=("arbitrary",), vmem_limit_bytes=mib * 1024 * 1024
    )


def cost(flops, moved):
    return pl.CostEstimate(flops=0, bytes_accessed=0, transcendentals=0)


def whole(shape):
    zeros = (0,) * len(shape)
    return pl.BlockSpec(shape, lambda *_: zeros)


def project_kernel(me_ref, x_ref, wk_ref, wv_ref, away_ref, keep_ref):
    other = pl.multiple_of((lax.rem(me_ref[0], 2) ^ 1) * HEAD_DIM, HEAD_DIM)
    for at, ref in ((other, away_ref), (HEAD_DIM - other, keep_ref)):
        span = pl.ds(pl.multiple_of(at, HEAD_DIM), HEAD_DIM)
        ref[...] = dot(x_ref[...], jnp.concatenate([wk_ref[:, span], wv_ref[:, span]], axis=1))


def project(me, x, w_key, w_value, far):
    rows, feats = x.shape
    step = rows // 2
    out = (rows, 2 * HEAD_DIM)
    weights = pl.BlockSpec((feats, 2 * HEAD_DIM), lambda i, me: (0, lax.div(me[0], 2) ^ far))
    block = pl.BlockSpec((step, 2 * HEAD_DIM), lambda i, me: (i, 0))
    spec = pltpu.PrefetchScalarGridSpec(
        num_scalar_prefetch=1,
        grid=(rows // step,),
        in_specs=[pl.BlockSpec((step, feats), lambda i, me: (i, 0)), weights, weights],
        out_specs=(block, block),
    )
    return pl.pallas_call(
        project_kernel,
        out_shape=(jax.ShapeDtypeStruct(out, F32),) * 2,
        grid_spec=spec,
        compiler_params=params(58),
        cost_estimate=cost(8 * rows * feats * HEAD_DIM, 5 << 20),
        name="project",
    )(me, x, w_key, w_value)


def slots_kernel(per, me_ref, dest_ref, len_ref, off_ref, x_ref, *refs):
    *xs_refs, pick_ref, meta_ref = refs
    samp = dest_ref.shape[1]
    rows, feats = x_ref.shape
    lmax = rows // samp
    row = dest_ref[...]
    a, b = iota((samp, samp), 0), iota((samp, samp), 1)
    col = jnp.sum(jnp.where(a == b, row, 0), axis=1, keepdims=True)
    rank = jnp.sum(jnp.where((col == row) & (a < b), 1, 0), axis=0, keepdims=True)
    slot = (row ^ me_ref[0]) * per + rank
    a, b = iota((samp, rows), 0), iota((samp, rows), 1)
    spread = (a == lax.div(b, lmax)).astype(BF16)
    wide = dot(jnp.broadcast_to(slot, (8, samp)).astype(BF16), spread)[0:1]
    source = wide.astype(I32) * lmax + lax.rem(iota((1, rows), 1), lmax)
    pick_ref[...] = (iota((rows, rows), 0) == source).astype(BF16)
    held = iota((samp, samp), 0) == slot
    size = jnp.sum(jnp.where(held, len_ref[...], 0), axis=1, keepdims=True)
    start = jnp.sum(jnp.where(held, off_ref[...], 0), axis=1, keepdims=True)
    lane = iota((samp, meta_ref.shape[2]), 1)
    table = jnp.where(lane == 0, size, jnp.where(lane == 2, lax.rem(start, lmax), 0))
    table = jnp.where(lane == 1, lax.div(start, lmax), table).astype(BF16)
    lines = meta_ref.shape[0] * meta_ref.shape[1]
    a, b = iota((lines, samp), 0), iota((lines, samp), 1)
    place = (b == lax.div(a, 16) * per + lax.rem(a, 16)) & (lax.rem(a, 16) < per)
    meta_ref[...] = dot(place.astype(BF16), table).astype(BF16).reshape(meta_ref.shape)
    part = xs_refs[0].shape[2]
    for f, ref in enumerate(xs_refs):
        for h in range(2):
            at = pl.multiple_of((me_ref[0] ^ (f + h * len(xs_refs))) * part, part)
            ref[h] = dot(pick_ref[...], x_ref[:, pl.ds(at, part)]).astype(BF16)


def slots(me, dest, lengths, offsets, x, learners, per):
    rows, feats = x.shape
    samp = dest.shape[0]
    part = feats // learners
    line = whole((1, samp))
    xs = ((2, rows, part),) * (learners // 2)
    outs = xs + ((rows, rows), (learners, 16, 2 * HEAD_DIM))
    spec = pltpu.PrefetchScalarGridSpec(
        num_scalar_prefetch=1,
        grid=(1,),
        in_specs=[line, line, line, whole((rows, feats))],
        out_specs=tuple(whole(o) for o in outs),
    )
    return pl.pallas_call(
        functools.partial(slots_kernel, per),
        out_shape=tuple(jax.ShapeDtypeStruct(o, BF16) for o in outs),
        grid_spec=spec,
        compiler_params=params(),
        cost_estimate=cost(2 * rows * rows * feats, 5 << 20),
        name="slots",
    )(me, dest.reshape(1, samp), lengths.reshape(1, samp), offsets.reshape(1, samp), x)


def pack_kernel(me_ref, mine_ref, core_ref, across_ref, pick_ref, meta_ref, *out_refs):
    total = (mine_ref[...] + core_ref[...]) + across_ref[...]
    placed = dot(pick_ref[...], total.astype(BF16)).astype(BF16)
    learners = meta_ref.shape[0]
    block = placed.shape[0] // learners
    for i in range(learners):
        ref = out_refs[0].at[me_ref[0] ^ i]
        ref[:block, :] = placed[i * block : (i + 1) * block]
        ref[block:, :] = meta_ref[i]


def pack(me, mine, core, across, pick, meta):
    rows, cols = across.shape
    learners, extra, _ = meta.shape
    out = (rows // learners + extra, cols)
    outs = ((learners,) + out,)
    part = whole((rows, cols))
    spec = pltpu.PrefetchScalarGridSpec(
        num_scalar_prefetch=1,
        grid=(1,),
        in_specs=[part, part, part, whole((rows, rows)), whole(meta.shape)],
        out_specs=tuple(whole(o) for o in outs),
    )
    return pl.pallas_call(
        pack_kernel,
        out_shape=tuple(jax.ShapeDtypeStruct(o, BF16) for o in outs),
        grid_spec=spec,
        compiler_params=params(),
        cost_estimate=cost(2 * rows * rows * cols, 3 << 20),
        name="pack",
    )(me, mine, core, across, pick, meta)


def attention_kernel(lmax, learners, half, me_ref, kv_ref, q_ref, g_ref, grad_ref, out_ref, place_ref):
    rows, cols = q_ref.shape
    block = rows // learners
    heads = cols // HEAD_DIM
    scale = 1.0 / HEAD_DIM**0.5
    count = learners // 2
    kv_refs = [kv_ref.at[me_ref[0] ^ (half * count + i)] for i in range(count)]
    lines = kv_ref.shape[1]
    meta = jnp.concatenate([ref[block:, :HEAD_DIM] for ref in kv_refs], axis=0)
    a, b = iota((rows // 2, meta.shape[0]), 0), iota((rows // 2, meta.shape[0]), 1)
    spread = (lax.div(a, block) * (lines - block) + lax.div(lax.rem(a, block), lmax) == b).astype(BF16)
    table = dot(spread, meta).astype(I32)
    inner = lax.rem(iota((rows // 2, 1), 0), lmax)
    alive = inner < table[:, 0:1]
    target = jnp.where(alive, table[:, 1:2] * lmax + table[:, 2:3] + inner, -1)
    place_ref[...] = (iota((rows // 2, rows), 1) == target).astype(BF16)
    size = HEAD_DIM
    a, b = iota((size, size), 0), iota((size, size), 1)
    near = (lax.div(a, lmax) == lax.div(b, lmax)) & (b <= a)
    for i in range(rows // 2 // size):
        span = slice(i * size, (i + 1) * size)
        first = i * size // block
        kv = jnp.concatenate([kv_refs[first + j][:block, :] for j in range(size // block)], axis=0)
        k, v = kv[:, :HEAD_DIM], kv[:, HEAD_DIM:]
        place = place_ref[span, :]
        q = dot(place, q_ref[...]).astype(BF16)
        g = dot(place, g_ref[...]).astype(BF16)
        q = jnp.concatenate([q[:, h * HEAD_DIM : (h + 1) * HEAD_DIM] for h in range(heads)], axis=0)
        g = jnp.concatenate([g[:, h * HEAD_DIM : (h + 1) * HEAD_DIM] for h in range(heads)], axis=0)
        allowed = jnp.tile(near & alive[span], (heads, 1))
        scores = jnp.where(allowed, dot(q, k, COLS_LAST) * scale, -1e30)
        top = jnp.max(scores, axis=1, keepdims=True)
        expo = jnp.exp(scores - top)
        total = jnp.sum(expo, axis=1, keepdims=True)
        probs = jnp.where(allowed, expo / total, 0.0)
        probs_b = probs.astype(BF16)
        out = dot(probs_b, v).astype(BF16)
        dprob = dot(g, v, COLS_LAST)
        delta = jnp.sum(g.astype(F32) * out.astype(F32), axis=1, keepdims=True)
        dscore_b = (probs * (dprob - delta)).astype(BF16)
        grad_ref[span, :HEAD_DIM] = (dot(dscore_b, q, ROWS_LAST) * scale).astype(BF16)
        grad_ref[span, HEAD_DIM:] = dot(probs_b, g, ROWS_LAST).astype(BF16)
        for h in range(heads):
            out_ref[span, h * HEAD_DIM : (h + 1) * HEAD_DIM] = out[h * size : (h + 1) * size]


def attention(me, kv, queries, out_grad, lmax, learners, half):
    rows, cols = queries.shape
    outs = ((rows // 2, 2 * HEAD_DIM), (rows // 2, cols), (rows // 2, rows))
    spec = pltpu.PrefetchScalarGridSpec(
        num_scalar_prefetch=1,
        grid=(1,),
        in_specs=[whole(kv.shape)] + [whole((rows, cols))] * 2,
        out_specs=tuple(whole(o) for o in outs),
    )
    return pl.pallas_call(
        functools.partial(attention_kernel, lmax, learners, half),
        out_shape=tuple(jax.ShapeDtypeStruct(o, BF16) for o in outs),
        grid_spec=spec,
        compiler_params=params(),
        cost_estimate=cost(4 * rows * rows * cols, 4 << 20),
        name="attention",
    )(me, kv, queries, out_grad)


def packed_rows_kernel(place0, place1, out0, out1, out_ref):
    total = dot(place0[...], out0[...], ROWS_LAST) + dot(place1[...], out1[...], ROWS_LAST)
    out_ref[...] = total.astype(BF16)


def packed_rows(place, outs):
    half, cols = outs[0].shape
    rows = place[0].shape[1]
    return pl.pallas_call(
        packed_rows_kernel,
        out_shape=jax.ShapeDtypeStruct((rows, cols), BF16),
        grid=(1,),
        in_specs=[whole((half, rows))] * 2 + [whole((half, cols))] * 2,
        out_specs=whole((rows, cols)),
        compiler_params=params(),
        cost_estimate=cost(4 * half * rows * cols, 3 << 20),
        name="packed_rows",
    )(*place, *outs)


def rows_kernel(me_ref, place0, place1, *refs):
    *g_refs, wk_ref, wv_ref, out_ref, grads = refs

    @pl.when(pl.program_id(0) == 0)
    def _():
        half = grads.shape[1] // 2
        for i in range(4):
            part = dot(place0[...], g_refs[2 * i][...], ROWS_LAST)
            part = (part + dot(place1[...], g_refs[2 * i + 1][...], ROWS_LAST)).astype(BF16)
            at = pl.multiple_of((me_ref[0] ^ i) * HEAD_DIM, HEAD_DIM)
            grads[:, pl.ds(at, HEAD_DIM)] = part[:, :HEAD_DIM]
            grads[:, pl.ds(at + half, HEAD_DIM)] = part[:, HEAD_DIM:]

    half = grads.shape[1] // 2
    total = dot(grads[:, :half], wk_ref[...], COLS_LAST)
    out_ref[...] = (total + dot(grads[:, half:], wv_ref[...], COLS_LAST)).astype(BF16)


def row_grads(me, place, parts, w_key, w_value):
    feats, cols = w_key.shape
    rows = place[0].shape[1]
    step = 512
    spec = pltpu.PrefetchScalarGridSpec(
        num_scalar_prefetch=1,
        grid=(feats // step,),
        in_specs=[whole((rows // 2, rows))] * 2
        + [whole((rows // 2, 2 * HEAD_DIM))] * 8
        + [pl.BlockSpec((step, cols), lambda i, me: (i, 0))] * 2,
        out_specs=pl.BlockSpec((rows, step), lambda i, me: (0, i)),
        scratch_shapes=[pltpu.VMEM((rows, 2 * cols), BF16)],
    )
    return pl.pallas_call(
        rows_kernel,
        out_shape=jax.ShapeDtypeStruct((rows, feats), BF16),
        grid_spec=spec,
        compiler_params=params(),
        cost_estimate=cost(4 * rows * feats * cols, 8 << 20),
        name="row_grads",
    )(me, *place, *parts, w_key, w_value)


def weights_kernel(x_refs, g_refs, out_refs):
    rows = x_refs[0].shape[1]
    group = len(x_refs) // 2
    block = rows // (2 * group)
    grads = []
    for f in range(group):
        g = [(g_refs[2 * (f ^ j) + b], j * block) for b in range(2) for j in range(group)]
        grads.append(jnp.concatenate([ref[at : at + block, :] for ref, at in g], axis=0))
    for side, out_ref in enumerate(out_refs):
        total = None
        for f, g in enumerate(grads):
            term = dot(x_refs[side * group + f][0], g, ROWS_LAST)
            total = term if total is None else total + term
        out_ref[...] = total.astype(out_ref.dtype)


def weight_grads(xs, pieces, half, dtype):
    _, rows, part = xs[0].shape
    out = (part, 2 * HEAD_DIM)

    def kernel(*refs):
        weights_kernel(refs[: len(xs)], refs[len(xs) : -2], refs[-2:])

    return pl.pallas_call(
        kernel,
        out_shape=(jax.ShapeDtypeStruct(out, dtype),) * 2,
        grid=(1,),
        in_specs=[pl.BlockSpec((1, rows, part), lambda i: (half, 0, 0))] * len(xs)
        + [whole(g.shape) for g in pieces],
        out_specs=(whole(out),) * 2,
        compiler_params=params(),
        cost_estimate=cost(4 * len(xs) * rows * part * HEAD_DIM, 6 << 20),
        name="weight_grads",
    )(*xs, *pieces)


def finish_kernel(learners, me_ref, *refs):
    *sums, k_ref, v_ref = refs
    for i in range(4):
        at = pl.ds(pl.multiple_of((me_ref[0] ^ i) * HEAD_DIM, HEAD_DIM), HEAD_DIM)
        total = (sums[2 * i][...] + sums[2 * i + 1][...].astype(F32)) / learners
        k_ref[:, at] = total[:, :HEAD_DIM]
        v_ref[:, at] = total[:, HEAD_DIM:]


def finish(me, sums, learners):
    part, cols = sums[0].shape
    out = (part, 2 * cols)
    spec = pltpu.PrefetchScalarGridSpec(
        num_scalar_prefetch=1,
        grid=(1,),
        in_specs=[whole((part, cols))] * 8,
        out_specs=(whole(out),) * 2,
    )
    return pl.pallas_call(
        functools.partial(finish_kernel, float(learners)),
        out_shape=(jax.ShapeDtypeStruct(out, F32),) * 2,
        grid_spec=spec,
        compiler_params=params(),
        cost_estimate=cost(part * cols, 2 << 20),
        name="finish",
    )(me, *sums)


def swap(x, axis, code):
    size = lax.axis_size(axis)
    return lax.ppermute(x, axis, [(i, i ^ code) for i in range(size)])


def after(x, *earlier):
    return lax.optimization_barrier((x,) + earlier)[0]


def local(roll_x, lengths, dest, offsets, queries, out_grad, w_key, w_value):
    learners, heads = lax.axis_size("dp"), lax.axis_size("mp")
    samp, lmax, feats = roll_x.shape
    per = (samp + learners - 1) // learners
    x = roll_x.reshape(samp * lmax, feats)
    m = lax.axis_index("mp").astype(I32).reshape(1)
    d = lax.axis_index("dp").astype(I32).reshape(1)

    away, keep = project(m, x, w_key, w_value, 1)
    core = swap(away, "mp", 1)
    *xs, pick, meta = slots(d, dest, lengths, offsets, after(x, away), learners, per)
    half = after(keep, pick) + core
    across = swap(half, "mp", 2)
    xs_core = [swap(after(xs[0], half), "mp", 1)]
    xs[1:3] = [swap(after(xs[f], half), "dp", f) for f in (1, 2)]
    xs[3] = swap(after(xs[3], xs[1], xs[2]), "dp", 3)
    away, keep = project(m, after(x, xs_core[0]), w_key, w_value, 0)
    core = swap(away, "mp", 1)
    kv = pack(d, keep, core, across, pick, meta)
    kv = lax.all_to_all(kv[0], "dp", split_axis=0, concat_axis=0, tiled=True)
    kv = after(kv, xs[3])

    beyond, out1, place1 = attention(d, kv, queries, out_grad, lmax, learners, 1)
    there = swap(beyond, "dp", 4)
    grads, out0, place0 = attention(d, after(kv, beyond), queries, out_grad, lmax, learners, 0)
    place = [place0, place1]

    xs = xs + xs_core + [swap(b, "mp", 1) for b in xs[1:]]
    near = {(0, 0, 0): grads, (0, 0, 1): there}
    hops = [
        ((0, 0), "dp", 1), ((0, 0), "dp", 2), ((0, 0), "mp", 2), ((2, 0), "dp", 1),
        ((1, 0), "mp", 2), ((0, 1), "dp", 2), ((1, 1), "dp", 2),
    ]
    for part in range(2):
        for (code, far), axis, step in hops:
            key = (code ^ step, far, part) if axis == "dp" else (code, 1 - far, part)
            near[key] = swap(near[code, far, part], axis, step)
    across = swap(beyond, "mp", 2)
    own = [grads, beyond, swap(grads, "mp", 1), swap(beyond, "mp", 1)]
    own += [near[0, 1, 0], across, swap(near[0, 1, 0], "mp", 1), swap(across, "mp", 1)]
    sums = [None] * 8
    for far in range(2):
        pieces = [near[c, far, b] for c in range(learners // 2) for b in range(2)]
        send = weight_grads(xs, pieces, 1, BF16)
        sums[4 * far + 1] = swap(send[0], "dp", 4)
        sums[4 * far + 3] = swap(send[1], ("dp", "mp"), 4 * heads + 1)
        sums[4 * far], keep = weight_grads(xs, pieces, 0, F32)
        sums[4 * far + 2] = swap(keep, "mp", 1)
    attn_out = packed_rows(place, [out0, out1])
    grad_x = row_grads(m, place, own, w_key, w_value)
    grad_wk, grad_wv = finish(m, sums, learners)
    return (attn_out, grad_x, grad_wk, grad_wv)


def solution(mesh):
    dp, mp = mesh.shape["dp"], mesh.shape["mp"]
    body = local if dp == 8 and mp == 4 else general
    return jax.shard_map(
        body,
        mesh=mesh,
        in_specs=(
            P("dp", None, "mp"),
            P("dp"),
            P("dp"),
            P("dp"),
            P("dp", "mp"),
            P("dp", "mp"),
            P("mp", None),
            P("mp", None),
        ),
        out_specs=(P("dp", "mp"), P("dp", "mp"), P(("mp", "dp"), None), P(("mp", "dp"), None)),
        check_vma=False,
    )
```

```python
import functools

import jax
import jax.numpy as jnp
from jax import lax
from jax.experimental import pallas as pl
from jax.experimental.pallas import tpu as pltpu
from jax.sharding import PartitionSpec as P

HEAD_DIM = 128


def attend(qs, ks, vs, grads, mask):
    scale = 1.0 / qs.shape[-1] ** 0.5
    scores = jnp.einsum("bqkge,bmke->bkgqm", qs, ks, preferred_element_type=jnp.float32) * scale
    allowed = mask[:, None, None, :, :]
    scores = jnp.where(allowed, scores, -1e30)
    top = jnp.max(scores, axis=-1, keepdims=True)
    expo = jnp.exp(scores - top)
    total = jnp.sum(expo, axis=-1, keepdims=True)
    probs = jnp.where(allowed, expo / total, 0.0)
    probs_b = probs.astype(jnp.bfloat16)
    out = jnp.einsum("bkgqm,bmke->bqkge", probs_b, vs, preferred_element_type=jnp.float32).astype(
        jnp.bfloat16
    )
    dprob = jnp.einsum("bqkge,bmke->bkgqm", grads, vs, preferred_element_type=jnp.float32)
    delta = jnp.einsum("bqkge,bqkge->bkgq", grads, out, preferred_element_type=jnp.float32)
    dscore = probs * (dprob - delta[..., None])
    dscore_b = dscore.astype(jnp.bfloat16)
    key_grad = (
        jnp.einsum("bkgqm,bqkge->bmke", dscore_b, qs, preferred_element_type=jnp.float32) * scale
    ).astype(jnp.bfloat16)
    val_grad = jnp.einsum(
        "bkgqm,bqkge->bmke", probs_b, grads, preferred_element_type=jnp.float32
    ).astype(jnp.bfloat16)
    return (out, key_grad, val_grad)


def input_grads(key_all, val_all, w_key, w_value):
    contract = (((1,), (1,)), ((), ()))
    total = lax.dot_general(key_all, w_key, contract, preferred_element_type=jnp.float32)
    total = total + lax.dot_general(val_all, w_value, contract, preferred_element_type=jnp.float32)
    return total.astype(jnp.bfloat16)


def general(roll_x, lengths, dest, offsets, queries, out_grad, w_key, w_value):
    learners = lax.axis_size("dp")
    samp, lmax, feats = roll_x.shape
    rows = queries.shape[0]
    slots_per = (samp + learners - 1) // learners
    slot_count = learners * slots_per
    order = jnp.arange(samp, dtype=jnp.int32)
    earlier = (dest[None, :] == dest[:, None]) & (order[None, :] < order[:, None])
    rank = jnp.sum(earlier.astype(jnp.int32), axis=1)
    slot = dest * slots_per + rank
    match = slot[None, :] == jnp.arange(slot_count, dtype=jnp.int32)[:, None]
    filled = jnp.any(match, axis=1)
    pick = jnp.sum(jnp.where(match, order[None, :], 0), axis=1)
    send_x = jnp.where(
        filled[:, None, None], jnp.take(roll_x, pick, axis=0), jnp.zeros((), jnp.bfloat16)
    )
    send_len = jnp.where(filled, jnp.take(lengths, pick), 0)
    send_off = jnp.where(filled, jnp.take(offsets, pick), 0)
    recv_x, recv_len, recv_off = (
        lax.all_to_all(send_x, "dp", split_axis=0, concat_axis=0, tiled=True),
        lax.all_to_all(send_len, "dp", split_axis=0, concat_axis=0, tiled=True),
        lax.all_to_all(send_off, "dp", split_axis=0, concat_axis=0, tiled=True),
    )
    position = jnp.arange(lmax, dtype=jnp.int32)
    live = position[None, :] < recv_len[:, None]
    target = jnp.where(live, recv_off[:, None] + position[None, :], rows).astype(jnp.int32)
    flat = target.reshape(-1)
    packed = (
        jnp.zeros((rows, feats), jnp.bfloat16).at[flat].set(recv_x.reshape(-1, feats), mode="drop")
    )
    part_k = jnp.dot(packed, w_key, preferred_element_type=jnp.float32)
    part_v = jnp.dot(packed, w_value, preferred_element_type=jnp.float32)
    key_mine, val_mine = (
        lax.psum_scatter(part_k, "mp", scatter_dimension=1, tiled=True),
        lax.psum_scatter(part_v, "mp", scatter_dimension=1, tiled=True),
    )
    keys = key_mine.astype(jnp.bfloat16)
    vals = val_mine.astype(jnp.bfloat16)
    local_heads = keys.shape[1] // HEAD_DIM
    q_cols = queries.shape[1]
    group = q_cols // (local_heads * HEAD_DIM)
    slot_ids = jnp.broadcast_to(
        jnp.arange(slot_count, dtype=jnp.int32)[:, None], (slot_count, lmax)
    )
    seg = jnp.full((rows,), -1, jnp.int32).at[flat].set(slot_ids.reshape(-1), mode="drop")
    rowpos = jnp.arange(rows, dtype=jnp.int32)
    mask = (
        (seg[:, None] == seg[None, :]) & (seg[:, None] >= 0) & (rowpos[None, :] <= rowpos[:, None])
    )
    out, key_grad, val_grad = attend(
        queries.reshape(1, rows, local_heads, group, HEAD_DIM),
        keys.reshape(1, rows, local_heads, HEAD_DIM),
        vals.reshape(1, rows, local_heads, HEAD_DIM),
        out_grad.reshape(1, rows, local_heads, group, HEAD_DIM),
        mask[None],
    )
    attn_out = out.reshape(rows, q_cols)
    key_grad = key_grad.reshape(rows, local_heads * HEAD_DIM)
    val_grad = val_grad.reshape(rows, local_heads * HEAD_DIM)
    key_all, val_all = (
        lax.all_gather(key_grad, "mp", axis=1, tiled=True),
        lax.all_gather(val_grad, "mp", axis=1, tiled=True),
    )
    grad_x = input_grads(key_all, val_all, w_key, w_value)
    contract = (((0,), (0,)), ((), ()))
    whole_k = lax.dot_general(packed, key_all, contract, preferred_element_type=jnp.float32)
    whole_v = lax.dot_general(packed, val_all, contract, preferred_element_type=jnp.float32)
    sum_k, sum_v = (
        lax.psum_scatter(whole_k, "dp", scatter_dimension=0, tiled=True),
        lax.psum_scatter(whole_v, "dp", scatter_dimension=0, tiled=True),
    )
    return (attn_out, grad_x, sum_k / learners, sum_v / learners)


BF16, F32, I32 = jnp.bfloat16, jnp.float32, jnp.int32
ROWS_LAST = (((0,), (0,)), ((), ()))
COLS_LAST = (((1,), (1,)), ((), ()))


def dot(a, b, dims=(((1,), (0,)), ((), ()))):
    return lax.dot_general(a, b, dims, preferred_element_type=F32)


def iota(shape, dim):
    return lax.broadcasted_iota(I32, shape, dim)


def params(mib=44):
    return pltpu.CompilerParams(
        dimension_semantics=("arbitrary",), vmem_limit_bytes=mib * 1024 * 1024
    )


def cost(flops, moved):
    return pl.CostEstimate(flops=0, bytes_accessed=0, transcendentals=0)


def whole(shape):
    zeros = (0,) * len(shape)
    return pl.BlockSpec(shape, lambda *_: zeros)


def project_kernel(me_ref, x_ref, wk_ref, wv_ref, away_ref, keep_ref):
    other = pl.multiple_of((lax.rem(me_ref[0], 2) ^ 1) * HEAD_DIM, HEAD_DIM)
    for at, ref in ((other, away_ref), (HEAD_DIM - other, keep_ref)):
        span = pl.ds(pl.multiple_of(at, HEAD_DIM), HEAD_DIM)
        ref[...] = dot(x_ref[...], jnp.concatenate([wk_ref[:, span], wv_ref[:, span]], axis=1))


def project(me, x, w_key, w_value, far):
    rows, feats = x.shape
    step = rows // 2
    out = (rows, 2 * HEAD_DIM)
    weights = pl.BlockSpec((feats, 2 * HEAD_DIM), lambda i, me: (0, lax.div(me[0], 2) ^ far))
    block = pl.BlockSpec((step, 2 * HEAD_DIM), lambda i, me: (i, 0))
    spec = pltpu.PrefetchScalarGridSpec(
        num_scalar_prefetch=1,
        grid=(rows // step,),
        in_specs=[pl.BlockSpec((step, feats), lambda i, me: (i, 0)), weights, weights],
        out_specs=(block, block),
    )
    return pl.pallas_call(
        project_kernel,
        out_shape=(jax.ShapeDtypeStruct(out, F32),) * 2,
        grid_spec=spec,
        compiler_params=params(58),
        cost_estimate=cost(8 * rows * feats * HEAD_DIM, 5 << 20),
        name="project",
    )(me, x, w_key, w_value)


def slots_kernel(per, me_ref, dest_ref, len_ref, off_ref, x_ref, *refs):
    *xs_refs, pick_ref, meta_ref = refs
    samp = dest_ref.shape[1]
    rows, feats = x_ref.shape
    lmax = rows // samp
    row = dest_ref[...]
    a, b = iota((samp, samp), 0), iota((samp, samp), 1)
    col = jnp.sum(jnp.where(a == b, row, 0), axis=1, keepdims=True)
    rank = jnp.sum(jnp.where((col == row) & (a < b), 1, 0), axis=0, keepdims=True)
    slot = (row ^ me_ref[0]) * per + rank
    a, b = iota((samp, rows), 0), iota((samp, rows), 1)
    spread = (a == lax.div(b, lmax)).astype(BF16)
    wide = dot(jnp.broadcast_to(slot, (8, samp)).astype(BF16), spread)[0:1]
    source = wide.astype(I32) * lmax + lax.rem(iota((1, rows), 1), lmax)
    pick_ref[...] = (iota((rows, rows), 0) == source).astype(BF16)
    held = iota((samp, samp), 0) == slot
    size = jnp.sum(jnp.where(held, len_ref[...], 0), axis=1, keepdims=True)
    start = jnp.sum(jnp.where(held, off_ref[...], 0), axis=1, keepdims=True)
    lane = iota((samp, meta_ref.shape[2]), 1)
    table = jnp.where(lane == 0, size, jnp.where(lane == 2, lax.rem(start, lmax), 0))
    table = jnp.where(lane == 1, lax.div(start, lmax), table).astype(BF16)
    lines = meta_ref.shape[0] * meta_ref.shape[1]
    a, b = iota((lines, samp), 0), iota((lines, samp), 1)
    place = (b == lax.div(a, 16) * per + lax.rem(a, 16)) & (lax.rem(a, 16) < per)
    meta_ref[...] = dot(place.astype(BF16), table).astype(BF16).reshape(meta_ref.shape)
    part = xs_refs[0].shape[2]
    for f, ref in enumerate(xs_refs):
        for h in range(2):
            at = pl.multiple_of((me_ref[0] ^ (f + h * len(xs_refs))) * part, part)
            ref[h] = dot(pick_ref[...], x_ref[:, pl.ds(at, part)]).astype(BF16)


def slots(me, dest, lengths, offsets, x, learners, per):
    rows, feats = x.shape
    samp = dest.shape[0]
    part = feats // learners
    line = whole((1, samp))
    xs = ((2, rows, part),) * (learners // 2)
    outs = xs + ((rows, rows), (learners, 16, 2 * HEAD_DIM))
    spec = pltpu.PrefetchScalarGridSpec(
        num_scalar_prefetch=1,
        grid=(1,),
        in_specs=[line, line, line, whole((rows, feats))],
        out_specs=tuple(whole(o) for o in outs),
    )
    return pl.pallas_call(
        functools.partial(slots_kernel, per),
        out_shape=tuple(jax.ShapeDtypeStruct(o, BF16) for o in outs),
        grid_spec=spec,
        compiler_params=params(),
        cost_estimate=cost(2 * rows * rows * feats, 5 << 20),
        name="slots",
    )(me, dest.reshape(1, samp), lengths.reshape(1, samp), offsets.reshape(1, samp), x)


def pack_kernel(me_ref, mine_ref, core_ref, across_ref, pick_ref, meta_ref, *out_refs):
    total = (mine_ref[...] + core_ref[...]) + across_ref[...]
    placed = dot(pick_ref[...], total.astype(BF16)).astype(BF16)
    learners = meta_ref.shape[0]
    block = placed.shape[0] // learners
    for i in range(learners):
        ref = out_refs[0].at[me_ref[0] ^ i]
        ref[:block, :] = placed[i * block : (i + 1) * block]
        ref[block:, :] = meta_ref[i]


def pack(me, mine, core, across, pick, meta):
    rows, cols = across.shape
    learners, extra, _ = meta.shape
    out = (rows // learners + extra, cols)
    outs = ((learners,) + out,)
    part = whole((rows, cols))
    spec = pltpu.PrefetchScalarGridSpec(
        num_scalar_prefetch=1,
        grid=(1,),
        in_specs=[part, part, part, whole((rows, rows)), whole(meta.shape)],
        out_specs=tuple(whole(o) for o in outs),
    )
    return pl.pallas_call(
        pack_kernel,
        out_shape=tuple(jax.ShapeDtypeStruct(o, BF16) for o in outs),
        grid_spec=spec,
        compiler_params=params(),
        cost_estimate=cost(2 * rows * rows * cols, 3 << 20),
        name="pack",
    )(me, mine, core, across, pick, meta)


def attention_kernel(lmax, learners, half, me_ref, kv_ref, q_ref, g_ref, grad_ref, out_ref, place_ref):
    rows, cols = q_ref.shape
    block = rows // learners
    heads = cols // HEAD_DIM
    scale = 1.0 / HEAD_DIM**0.5
    count = learners // 2
    kv_refs = [kv_ref.at[me_ref[0] ^ (half * count + i)] for i in range(count)]
    lines = kv_ref.shape[1]
    meta = jnp.concatenate([ref[block:, :HEAD_DIM] for ref in kv_refs], axis=0)
    a, b = iota((rows // 2, meta.shape[0]), 0), iota((rows // 2, meta.shape[0]), 1)
    spread = (lax.div(a, block) * (lines - block) + lax.div(lax.rem(a, block), lmax) == b).astype(BF16)
    table = dot(spread, meta).astype(I32)
    inner = lax.rem(iota((rows // 2, 1), 0), lmax)
    alive = inner < table[:, 0:1]
    target = jnp.where(alive, table[:, 1:2] * lmax + table[:, 2:3] + inner, -1)
    place_ref[...] = (iota((rows // 2, rows), 1) == target).astype(BF16)
    size = HEAD_DIM
    a, b = iota((size, size), 0), iota((size, size), 1)
    near = (lax.div(a, lmax) == lax.div(b, lmax)) & (b <= a)
    for i in range(rows // 2 // size):
        span = slice(i * size, (i + 1) * size)
        first = i * size // block
        kv = jnp.concatenate([kv_refs[first + j][:block, :] for j in range(size // block)], axis=0)
        k, v = kv[:, :HEAD_DIM], kv[:, HEAD_DIM:]
        place = place_ref[span, :]
        q = dot(place, q_ref[...]).astype(BF16)
        g = dot(place, g_ref[...]).astype(BF16)
        q = jnp.concatenate([q[:, h * HEAD_DIM : (h + 1) * HEAD_DIM] for h in range(heads)], axis=0)
        g = jnp.concatenate([g[:, h * HEAD_DIM : (h + 1) * HEAD_DIM] for h in range(heads)], axis=0)
        allowed = jnp.tile(near & alive[span], (heads, 1))
        scores = jnp.where(allowed, dot(q, k, COLS_LAST) * scale, -1e30)
        top = jnp.max(scores, axis=1, keepdims=True)
        expo = jnp.exp(scores - top)
        total = jnp.sum(expo, axis=1, keepdims=True)
        probs = jnp.where(allowed, expo / total, 0.0)
        probs_b = probs.astype(BF16)
        out = dot(probs_b, v).astype(BF16)
        dprob = dot(g, v, COLS_LAST)
        delta = jnp.sum(g.astype(F32) * out.astype(F32), axis=1, keepdims=True)
        dscore_b = (probs * (dprob - delta)).astype(BF16)
        grad_ref[span, :HEAD_DIM] = (dot(dscore_b, q, ROWS_LAST) * scale).astype(BF16)
        grad_ref[span, HEAD_DIM:] = dot(probs_b, g, ROWS_LAST).astype(BF16)
        for h in range(heads):
            out_ref[span, h * HEAD_DIM : (h + 1) * HEAD_DIM] = out[h * size : (h + 1) * size]


def attention(me, kv, queries, out_grad, lmax, learners, half):
    rows, cols = queries.shape
    outs = ((rows // 2, 2 * HEAD_DIM), (rows // 2, cols), (rows // 2, rows))
    spec = pltpu.PrefetchScalarGridSpec(
        num_scalar_prefetch=1,
        grid=(1,),
        in_specs=[whole(kv.shape)] + [whole((rows, cols))] * 2,
        out_specs=tuple(whole(o) for o in outs),
    )
    return pl.pallas_call(
        functools.partial(attention_kernel, lmax, learners, half),
        out_shape=tuple(jax.ShapeDtypeStruct(o, BF16) for o in outs),
        grid_spec=spec,
        compiler_params=params(),
        cost_estimate=cost(4 * rows * rows * cols, 4 << 20),
        name="attention",
    )(me, kv, queries, out_grad)


def packed_rows_kernel(place0, place1, out0, out1, out_ref):
    total = dot(place0[...], out0[...], ROWS_LAST) + dot(place1[...], out1[...], ROWS_LAST)
    out_ref[...] = total.astype(BF16)


def packed_rows(place, outs):
    half, cols = outs[0].shape
    rows = place[0].shape[1]
    return pl.pallas_call(
        packed_rows_kernel,
        out_shape=jax.ShapeDtypeStruct((rows, cols), BF16),
        grid=(1,),
        in_specs=[whole((half, rows))] * 2 + [whole((half, cols))] * 2,
        out_specs=whole((rows, cols)),
        compiler_params=params(),
        cost_estimate=cost(4 * half * rows * cols, 3 << 20),
        name="packed_rows",
    )(*place, *outs)


def rows_kernel(me_ref, place0, place1, *refs):
    *g_refs, wk_ref, wv_ref, out_ref, grads = refs

    @pl.when(pl.program_id(0) == 0)
    def _():
        half = grads.shape[1] // 2
        for i in range(4):
            part = dot(place0[...], g_refs[2 * i][...], ROWS_LAST)
            part = (part + dot(place1[...], g_refs[2 * i + 1][...], ROWS_LAST)).astype(BF16)
            at = pl.multiple_of((me_ref[0] ^ i) * HEAD_DIM, HEAD_DIM)
            grads[:, pl.ds(at, HEAD_DIM)] = part[:, :HEAD_DIM]
            grads[:, pl.ds(at + half, HEAD_DIM)] = part[:, HEAD_DIM:]

    half = grads.shape[1] // 2
    total = dot(grads[:, :half], wk_ref[...], COLS_LAST)
    out_ref[...] = (total + dot(grads[:, half:], wv_ref[...], COLS_LAST)).astype(BF16)


def row_grads(me, place, parts, w_key, w_value):
    feats, cols = w_key.shape
    rows = place[0].shape[1]
    step = 512
    spec = pltpu.PrefetchScalarGridSpec(
        num_scalar_prefetch=1,
        grid=(feats // step,),
        in_specs=[whole((rows // 2, rows))] * 2
        + [whole((rows // 2, 2 * HEAD_DIM))] * 8
        + [pl.BlockSpec((step, cols), lambda i, me: (i, 0))] * 2,
        out_specs=pl.BlockSpec((rows, step), lambda i, me: (0, i)),
        scratch_shapes=[pltpu.VMEM((rows, 2 * cols), BF16)],
    )
    return pl.pallas_call(
        rows_kernel,
        out_shape=jax.ShapeDtypeStruct((rows, feats), BF16),
        grid_spec=spec,
        compiler_params=params(),
        cost_estimate=cost(4 * rows * feats * cols, 8 << 20),
        name="row_grads",
    )(me, *place, *parts, w_key, w_value)


def weights_kernel(x_refs, g_refs, out_refs):
    rows = x_refs[0].shape[1]
    group = len(x_refs) // 2
    block = rows // (2 * group)
    grads = []
    for f in range(group):
        g = [(g_refs[2 * (f ^ j) + b], j * block) for b in range(2) for j in range(group)]
        grads.append(jnp.concatenate([ref[at : at + block, :] for ref, at in g], axis=0))
    for side, out_ref in enumerate(out_refs):
        total = None
        for f, g in enumerate(grads):
            term = dot(x_refs[side * group + f][0], g, ROWS_LAST)
            total = term if total is None else total + term
        out_ref[...] = total.astype(out_ref.dtype)


def weight_grads(xs, pieces, half, dtype):
    _, rows, part = xs[0].shape
    out = (part, 2 * HEAD_DIM)

    def kernel(*refs):
        weights_kernel(refs[: len(xs)], refs[len(xs) : -2], refs[-2:])

    return pl.pallas_call(
        kernel,
        out_shape=(jax.ShapeDtypeStruct(out, dtype),) * 2,
        grid=(1,),
        in_specs=[pl.BlockSpec((1, rows, part), lambda i: (half, 0, 0))] * len(xs)
        + [whole(g.shape) for g in pieces],
        out_specs=(whole(out),) * 2,
        compiler_params=params(),
        cost_estimate=cost(4 * len(xs) * rows * part * HEAD_DIM, 6 << 20),
        name="weight_grads",
    )(*xs, *pieces)


def finish_kernel(learners, me_ref, *refs):
    *sums, k_ref, v_ref = refs
    for i in range(4):
        at = pl.ds(pl.multiple_of((me_ref[0] ^ i) * HEAD_DIM, HEAD_DIM), HEAD_DIM)
        total = (sums[2 * i][...] + sums[2 * i + 1][...].astype(F32)) / learners
        k_ref[:, at] = total[:, :HEAD_DIM]
        v_ref[:, at] = total[:, HEAD_DIM:]


def finish(me, sums, learners):
    part, cols = sums[0].shape
    out = (part, 2 * cols)
    spec = pltpu.PrefetchScalarGridSpec(
        num_scalar_prefetch=1,
        grid=(1,),
        in_specs=[whole((part, cols))] * 8,
        out_specs=(whole(out),) * 2,
    )
    return pl.pallas_call(
        functools.partial(finish_kernel, float(learners)),
        out_shape=(jax.ShapeDtypeStruct(out, F32),) * 2,
        grid_spec=spec,
        compiler_params=params(),
        cost_estimate=cost(part * cols, 2 << 20),
        name="finish",
    )(me, *sums)


def swap(x, axis, code):
    size = lax.axis_size(axis)
    return lax.ppermute(x, axis, [(i, i ^ code) for i in range(size)])


def after(x, *earlier):
    return lax.optimization_barrier((x,) + earlier)[0]


def local(roll_x, lengths, dest, offsets, queries, out_grad, w_key, w_value):
    learners, heads = lax.axis_size("dp"), lax.axis_size("mp")
    samp, lmax, feats = roll_x.shape
    per = (samp + learners - 1) // learners
    x = roll_x.reshape(samp * lmax, feats)
    m = lax.axis_index("mp").astype(I32).reshape(1)
    d = lax.axis_index("dp").astype(I32).reshape(1)

    away, keep = project(m, x, w_key, w_value, 1)
    core = swap(away, "mp", 1)
    *xs, pick, meta = slots(d, dest, lengths, offsets, after(x, away), learners, per)
    half = after(keep, pick) + core
    across = swap(half, "mp", 2)
    xs_core = [swap(after(xs[0], half), "mp", 1)]
    xs[1:3] = [swap(after(xs[f], half), "dp", f) for f in (1, 2)]
    xs[3] = swap(after(xs[3], xs[1], xs[2]), "dp", 3)
    away, keep = project(m, after(x, xs_core[0]), w_key, w_value, 0)
    core = swap(away, "mp", 1)
    kv = pack(d, keep, core, across, pick, meta)
    kv = lax.all_to_all(kv[0], "dp", split_axis=0, concat_axis=0, tiled=True)
    kv = after(kv, xs[3])

    beyond, out1, place1 = attention(d, kv, queries, out_grad, lmax, learners, 1)
    there = swap(beyond, "dp", 4)
    grads, out0, place0 = attention(d, after(kv, beyond), queries, out_grad, lmax, learners, 0)
    place = [place0, place1]

    xs = xs + xs_core + [swap(b, "mp", 1) for b in xs[1:]]
    near = {(0, 0, 0): grads, (0, 0, 1): there}
    hops = [
        [
            (0, 0, "dp", 1),
            (0, 0, "dp", 2),
            (0, 0, "mp", 2),
            (2, 0, "dp", 1),
            (1, 0, "mp", 2),
            (0, 1, "dp", 2),
            (2, 1, "dp", 1),
        ],
        [
            (0, 0, "dp", 1),
            (0, 0, "dp", 2),
            (0, 0, "mp", 2),
            (2, 0, "dp", 1),
            (1, 0, "mp", 2),
            (0, 1, "dp", 2),
            (1, 1, "dp", 2),
        ],
    ]
    for part, plan in enumerate((hops[0], hops[1])):
        for code, far, axis, step in plan:
            key = (code ^ step, far, part) if axis == "dp" else (code, 1 - far, part)
            near[key] = swap(near[code, far, part], axis, step)
    across = swap(beyond, "mp", 2)
    own = [grads, beyond, swap(grads, "mp", 1), swap(beyond, "mp", 1)]
    own += [near[0, 1, 0], across, swap(near[0, 1, 0], "mp", 1), swap(across, "mp", 1)]
    sums = [None] * 8
    for far in range(2):
        pieces = [near[c, far, b] for c in range(learners // 2) for b in range(2)]
        send = weight_grads(xs, pieces, 1, BF16)
        sums[4 * far + 1] = swap(send[0], "dp", 4)
        sums[4 * far + 3] = swap(send[1], ("dp", "mp"), 4 * heads + 1)
        sums[4 * far], keep = weight_grads(xs, pieces, 0, F32)
        sums[4 * far + 2] = swap(keep, "mp", 1)
    attn_out = packed_rows(place, [out0, out1])
    grad_x = row_grads(m, place, own, w_key, w_value)
    grad_wk, grad_wv = finish(m, sums, learners)
    return (attn_out, grad_x, grad_wk, grad_wv)


def solution(mesh):
    dp, mp = mesh.shape["dp"], mesh.shape["mp"]
    body = local if dp == 8 and mp == 4 else general
    return jax.shard_map(
        body,
        mesh=mesh,
        in_specs=(
            P("dp", None, "mp"),
            P("dp"),
            P("dp"),
            P("dp"),
            P("dp", "mp"),
            P("dp", "mp"),
            P("mp", None),
            P("mp", None),
        ),
        out_specs=(P("dp", "mp"), P("dp", "mp"), P(("mp", "dp"), None), P(("mp", "dp"), None)),
        check_vma=False,
    )
```

```python
import functools

import jax
import jax.numpy as jnp
from jax import lax
from jax.experimental import pallas as pl
from jax.experimental.pallas import tpu as pltpu
from jax.sharding import PartitionSpec as P

HEAD_DIM = 128


def attend(qs, ks, vs, grads, mask):
    scale = 1.0 / qs.shape[-1] ** 0.5
    scores = jnp.einsum("bqkge,bmke->bkgqm", qs, ks, preferred_element_type=jnp.float32) * scale
    allowed = mask[:, None, None, :, :]
    scores = jnp.where(allowed, scores, -1e30)
    top = jnp.max(scores, axis=-1, keepdims=True)
    expo = jnp.exp(scores - top)
    total = jnp.sum(expo, axis=-1, keepdims=True)
    probs = jnp.where(allowed, expo / total, 0.0)
    probs_b = probs.astype(jnp.bfloat16)
    out = jnp.einsum("bkgqm,bmke->bqkge", probs_b, vs, preferred_element_type=jnp.float32).astype(
        jnp.bfloat16
    )
    dprob = jnp.einsum("bqkge,bmke->bkgqm", grads, vs, preferred_element_type=jnp.float32)
    delta = jnp.einsum("bqkge,bqkge->bkgq", grads, out, preferred_element_type=jnp.float32)
    dscore = probs * (dprob - delta[..., None])
    dscore_b = dscore.astype(jnp.bfloat16)
    key_grad = (
        jnp.einsum("bkgqm,bqkge->bmke", dscore_b, qs, preferred_element_type=jnp.float32) * scale
    ).astype(jnp.bfloat16)
    val_grad = jnp.einsum(
        "bkgqm,bqkge->bmke", probs_b, grads, preferred_element_type=jnp.float32
    ).astype(jnp.bfloat16)
    return (out, key_grad, val_grad)


def input_grads(key_all, val_all, w_key, w_value):
    contract = (((1,), (1,)), ((), ()))
    total = lax.dot_general(key_all, w_key, contract, preferred_element_type=jnp.float32)
    total = total + lax.dot_general(val_all, w_value, contract, preferred_element_type=jnp.float32)
    return total.astype(jnp.bfloat16)


def general(roll_x, lengths, dest, offsets, queries, out_grad, w_key, w_value):
    learners = lax.axis_size("dp")
    samp, lmax, feats = roll_x.shape
    rows = queries.shape[0]
    slots_per = (samp + learners - 1) // learners
    slot_count = learners * slots_per
    order = jnp.arange(samp, dtype=jnp.int32)
    earlier = (dest[None, :] == dest[:, None]) & (order[None, :] < order[:, None])
    rank = jnp.sum(earlier.astype(jnp.int32), axis=1)
    slot = dest * slots_per + rank
    match = slot[None, :] == jnp.arange(slot_count, dtype=jnp.int32)[:, None]
    filled = jnp.any(match, axis=1)
    pick = jnp.sum(jnp.where(match, order[None, :], 0), axis=1)
    send_x = jnp.where(
        filled[:, None, None], jnp.take(roll_x, pick, axis=0), jnp.zeros((), jnp.bfloat16)
    )
    send_len = jnp.where(filled, jnp.take(lengths, pick), 0)
    send_off = jnp.where(filled, jnp.take(offsets, pick), 0)
    recv_x, recv_len, recv_off = (
        lax.all_to_all(send_x, "dp", split_axis=0, concat_axis=0, tiled=True),
        lax.all_to_all(send_len, "dp", split_axis=0, concat_axis=0, tiled=True),
        lax.all_to_all(send_off, "dp", split_axis=0, concat_axis=0, tiled=True),
    )
    position = jnp.arange(lmax, dtype=jnp.int32)
    live = position[None, :] < recv_len[:, None]
    target = jnp.where(live, recv_off[:, None] + position[None, :], rows).astype(jnp.int32)
    flat = target.reshape(-1)
    packed = (
        jnp.zeros((rows, feats), jnp.bfloat16).at[flat].set(recv_x.reshape(-1, feats), mode="drop")
    )
    part_k = jnp.dot(packed, w_key, preferred_element_type=jnp.float32)
    part_v = jnp.dot(packed, w_value, preferred_element_type=jnp.float32)
    key_mine, val_mine = (
        lax.psum_scatter(part_k, "mp", scatter_dimension=1, tiled=True),
        lax.psum_scatter(part_v, "mp", scatter_dimension=1, tiled=True),
    )
    keys = key_mine.astype(jnp.bfloat16)
    vals = val_mine.astype(jnp.bfloat16)
    local_heads = keys.shape[1] // HEAD_DIM
    q_cols = queries.shape[1]
    group = q_cols // (local_heads * HEAD_DIM)
    slot_ids = jnp.broadcast_to(
        jnp.arange(slot_count, dtype=jnp.int32)[:, None], (slot_count, lmax)
    )
    seg = jnp.full((rows,), -1, jnp.int32).at[flat].set(slot_ids.reshape(-1), mode="drop")
    rowpos = jnp.arange(rows, dtype=jnp.int32)
    mask = (
        (seg[:, None] == seg[None, :]) & (seg[:, None] >= 0) & (rowpos[None, :] <= rowpos[:, None])
    )
    out, key_grad, val_grad = attend(
        queries.reshape(1, rows, local_heads, group, HEAD_DIM),
        keys.reshape(1, rows, local_heads, HEAD_DIM),
        vals.reshape(1, rows, local_heads, HEAD_DIM),
        out_grad.reshape(1, rows, local_heads, group, HEAD_DIM),
        mask[None],
    )
    attn_out = out.reshape(rows, q_cols)
    key_grad = key_grad.reshape(rows, local_heads * HEAD_DIM)
    val_grad = val_grad.reshape(rows, local_heads * HEAD_DIM)
    key_all, val_all = (
        lax.all_gather(key_grad, "mp", axis=1, tiled=True),
        lax.all_gather(val_grad, "mp", axis=1, tiled=True),
    )
    grad_x = input_grads(key_all, val_all, w_key, w_value)
    contract = (((0,), (0,)), ((), ()))
    whole_k = lax.dot_general(packed, key_all, contract, preferred_element_type=jnp.float32)
    whole_v = lax.dot_general(packed, val_all, contract, preferred_element_type=jnp.float32)
    sum_k, sum_v = (
        lax.psum_scatter(whole_k, "dp", scatter_dimension=0, tiled=True),
        lax.psum_scatter(whole_v, "dp", scatter_dimension=0, tiled=True),
    )
    return (attn_out, grad_x, sum_k / learners, sum_v / learners)


BF16, F32, I32 = jnp.bfloat16, jnp.float32, jnp.int32
ROWS_LAST = (((0,), (0,)), ((), ()))
COLS_LAST = (((1,), (1,)), ((), ()))


def dot(a, b, dims=(((1,), (0,)), ((), ()))):
    return lax.dot_general(a, b, dims, preferred_element_type=F32)


def iota(shape, dim):
    return lax.broadcasted_iota(I32, shape, dim)


def params(mib=44):
    return pltpu.CompilerParams(
        dimension_semantics=("arbitrary",), vmem_limit_bytes=mib * 1024 * 1024
    )


def cost(flops, moved):
    return pl.CostEstimate(flops=0, bytes_accessed=0, transcendentals=0)


def whole(shape):
    zeros = (0,) * len(shape)
    return pl.BlockSpec(shape, lambda *_: zeros)


def project_kernel(me_ref, x_ref, wk_ref, wv_ref, away_ref, keep_ref):
    other = pl.multiple_of((lax.rem(me_ref[0], 2) ^ 1) * HEAD_DIM, HEAD_DIM)
    for at, ref in ((other, away_ref), (HEAD_DIM - other, keep_ref)):
        span = pl.ds(pl.multiple_of(at, HEAD_DIM), HEAD_DIM)
        ref[...] = dot(x_ref[...], jnp.concatenate([wk_ref[:, span], wv_ref[:, span]], axis=1))


def project(me, x, w_key, w_value, far):
    rows, feats = x.shape
    step = rows // 2
    out = (rows, 2 * HEAD_DIM)
    weights = pl.BlockSpec((feats, 2 * HEAD_DIM), lambda i, me: (0, lax.div(me[0], 2) ^ far))
    block = pl.BlockSpec((step, 2 * HEAD_DIM), lambda i, me: (i, 0))
    spec = pltpu.PrefetchScalarGridSpec(
        num_scalar_prefetch=1,
        grid=(rows // step,),
        in_specs=[pl.BlockSpec((step, feats), lambda i, me: (i, 0)), weights, weights],
        out_specs=(block, block),
    )
    return pl.pallas_call(
        project_kernel,
        out_shape=(jax.ShapeDtypeStruct(out, F32),) * 2,
        grid_spec=spec,
        compiler_params=params(58),
        cost_estimate=cost(8 * rows * feats * HEAD_DIM, 5 << 20),
        name="project",
    )(me, x, w_key, w_value)


def slots_kernel(per, me_ref, dest_ref, len_ref, off_ref, x_ref, *refs):
    *xs_refs, pick_ref, meta_ref = refs
    samp = dest_ref.shape[1]
    rows, feats = x_ref.shape
    lmax = rows // samp
    row = dest_ref[...]
    a, b = iota((samp, samp), 0), iota((samp, samp), 1)
    col = jnp.sum(jnp.where(a == b, row, 0), axis=1, keepdims=True)
    rank = jnp.sum(jnp.where((col == row) & (a < b), 1, 0), axis=0, keepdims=True)
    slot = (row ^ me_ref[0]) * per + rank
    a, b = iota((samp, rows), 0), iota((samp, rows), 1)
    spread = (a == lax.div(b, lmax)).astype(BF16)
    wide = dot(jnp.broadcast_to(slot, (8, samp)).astype(BF16), spread)[0:1]
    source = wide.astype(I32) * lmax + lax.rem(iota((1, rows), 1), lmax)
    pick_ref[...] = (iota((rows, rows), 0) == source).astype(BF16)
    held = iota((samp, samp), 0) == slot
    size = jnp.sum(jnp.where(held, len_ref[...], 0), axis=1, keepdims=True)
    start = jnp.sum(jnp.where(held, off_ref[...], 0), axis=1, keepdims=True)
    lane = iota((samp, meta_ref.shape[2]), 1)
    table = jnp.where(lane == 0, size, jnp.where(lane == 2, lax.rem(start, lmax), 0))
    table = jnp.where(lane == 1, lax.div(start, lmax), table).astype(BF16)
    lines = meta_ref.shape[0] * meta_ref.shape[1]
    a, b = iota((lines, samp), 0), iota((lines, samp), 1)
    place = (b == lax.div(a, 16) * per + lax.rem(a, 16)) & (lax.rem(a, 16) < per)
    meta_ref[...] = dot(place.astype(BF16), table).astype(BF16).reshape(meta_ref.shape)
    part = xs_refs[0].shape[2]
    for f, ref in enumerate(xs_refs):
        for h in range(2):
            at = pl.multiple_of((me_ref[0] ^ (f + h * len(xs_refs))) * part, part)
            ref[h] = dot(pick_ref[...], x_ref[:, pl.ds(at, part)]).astype(BF16)


def slots(me, dest, lengths, offsets, x, learners, per):
    rows, feats = x.shape
    samp = dest.shape[0]
    part = feats // learners
    line = whole((1, samp))
    xs = ((2, rows, part),) * (learners // 2)
    outs = xs + ((rows, rows), (learners, 16, 2 * HEAD_DIM))
    spec = pltpu.PrefetchScalarGridSpec(
        num_scalar_prefetch=1,
        grid=(1,),
        in_specs=[line, line, line, whole((rows, feats))],
        out_specs=tuple(whole(o) for o in outs),
    )
    return pl.pallas_call(
        functools.partial(slots_kernel, per),
        out_shape=tuple(jax.ShapeDtypeStruct(o, BF16) for o in outs),
        grid_spec=spec,
        compiler_params=params(26),
        cost_estimate=cost(2 * rows * rows * feats, 5 << 20),
        name="slots",
    )(me, dest.reshape(1, samp), lengths.reshape(1, samp), offsets.reshape(1, samp), x)


def pack_kernel(me_ref, mine_ref, core_ref, across_ref, pick_ref, meta_ref, *out_refs):
    total = (mine_ref[...] + core_ref[...]) + across_ref[...]
    placed = dot(pick_ref[...], total.astype(BF16)).astype(BF16)
    learners = meta_ref.shape[0]
    block = placed.shape[0] // learners
    for i in range(learners):
        ref = out_refs[0].at[me_ref[0] ^ i]
        ref[:block, :] = placed[i * block : (i + 1) * block]
        ref[block:, :] = meta_ref[i]


def pack(me, mine, core, across, pick, meta):
    rows, cols = across.shape
    learners, extra, _ = meta.shape
    out = (rows // learners + extra, cols)
    outs = ((learners,) + out,)
    part = whole((rows, cols))
    spec = pltpu.PrefetchScalarGridSpec(
        num_scalar_prefetch=1,
        grid=(1,),
        in_specs=[part, part, part, whole((rows, rows)), whole(meta.shape)],
        out_specs=tuple(whole(o) for o in outs),
    )
    return pl.pallas_call(
        pack_kernel,
        out_shape=tuple(jax.ShapeDtypeStruct(o, BF16) for o in outs),
        grid_spec=spec,
        compiler_params=params(16),
        cost_estimate=cost(2 * rows * rows * cols, 3 << 20),
        name="pack",
    )(me, mine, core, across, pick, meta)


def attention_kernel(lmax, learners, half, me_ref, kv_ref, q_ref, g_ref, grad_ref, out_ref, place_ref):
    rows, cols = q_ref.shape
    block = rows // learners
    heads = cols // HEAD_DIM
    scale = 1.0 / HEAD_DIM**0.5
    count = learners // 2
    kv_refs = [kv_ref.at[me_ref[0] ^ (half * count + i)] for i in range(count)]
    lines = kv_ref.shape[1]
    meta = jnp.concatenate([ref[block:, :HEAD_DIM] for ref in kv_refs], axis=0)
    a, b = iota((rows // 2, meta.shape[0]), 0), iota((rows // 2, meta.shape[0]), 1)
    spread = (lax.div(a, block) * (lines - block) + lax.div(lax.rem(a, block), lmax) == b).astype(BF16)
    table = dot(spread, meta).astype(I32)
    inner = lax.rem(iota((rows // 2, 1), 0), lmax)
    alive = inner < table[:, 0:1]
    target = jnp.where(alive, table[:, 1:2] * lmax + table[:, 2:3] + inner, -1)
    place_ref[...] = (iota((rows // 2, rows), 1) == target).astype(BF16)
    size = HEAD_DIM
    a, b = iota((size, size), 0), iota((size, size), 1)
    near = (lax.div(a, lmax) == lax.div(b, lmax)) & (b <= a)
    for i in range(rows // 2 // size):
        span = slice(i * size, (i + 1) * size)
        first = i * size // block
        kv = jnp.concatenate([kv_refs[first + j][:block, :] for j in range(size // block)], axis=0)
        k, v = kv[:, :HEAD_DIM], kv[:, HEAD_DIM:]
        place = place_ref[span, :]
        q = dot(place, q_ref[...]).astype(BF16)
        g = dot(place, g_ref[...]).astype(BF16)
        q = jnp.concatenate([q[:, h * HEAD_DIM : (h + 1) * HEAD_DIM] for h in range(heads)], axis=0)
        g = jnp.concatenate([g[:, h * HEAD_DIM : (h + 1) * HEAD_DIM] for h in range(heads)], axis=0)
        allowed = jnp.tile(near & alive[span], (heads, 1))
        scores = jnp.where(allowed, dot(q, k, COLS_LAST) * scale, -1e30)
        top = jnp.max(scores, axis=1, keepdims=True)
        expo = jnp.exp(scores - top)
        total = jnp.sum(expo, axis=1, keepdims=True)
        probs = jnp.where(allowed, expo / total, 0.0)
        probs_b = probs.astype(BF16)
        out = dot(probs_b, v).astype(BF16)
        dprob = dot(g, v, COLS_LAST)
        delta = jnp.sum(g.astype(F32) * out.astype(F32), axis=1, keepdims=True)
        dscore_b = (probs * (dprob - delta)).astype(BF16)
        grad_ref[span, :HEAD_DIM] = (dot(dscore_b, q, ROWS_LAST) * scale).astype(BF16)
        grad_ref[span, HEAD_DIM:] = dot(probs_b, g, ROWS_LAST).astype(BF16)
        for h in range(heads):
            out_ref[span, h * HEAD_DIM : (h + 1) * HEAD_DIM] = out[h * size : (h + 1) * size]


def attention(me, kv, queries, out_grad, lmax, learners, half):
    rows, cols = queries.shape
    outs = ((rows // 2, 2 * HEAD_DIM), (rows // 2, cols), (rows // 2, rows))
    spec = pltpu.PrefetchScalarGridSpec(
        num_scalar_prefetch=1,
        grid=(1,),
        in_specs=[whole(kv.shape)] + [whole((rows, cols))] * 2,
        out_specs=tuple(whole(o) for o in outs),
    )
    return pl.pallas_call(
        functools.partial(attention_kernel, lmax, learners, half),
        out_shape=tuple(jax.ShapeDtypeStruct(o, BF16) for o in outs),
        grid_spec=spec,
        compiler_params=params(30),
        cost_estimate=cost(4 * rows * rows * cols, 4 << 20),
        name="attention",
    )(me, kv, queries, out_grad)


def packed_rows_kernel(place0, place1, out0, out1, out_ref):
    total = dot(place0[...], out0[...], ROWS_LAST) + dot(place1[...], out1[...], ROWS_LAST)
    out_ref[...] = total.astype(BF16)


def packed_rows(place, outs):
    half, cols = outs[0].shape
    rows = place[0].shape[1]
    return pl.pallas_call(
        packed_rows_kernel,
        out_shape=jax.ShapeDtypeStruct((rows, cols), BF16),
        grid=(1,),
        in_specs=[whole((half, rows))] * 2 + [whole((half, cols))] * 2,
        out_specs=whole((rows, cols)),
        compiler_params=params(16),
        cost_estimate=cost(4 * half * rows * cols, 3 << 20),
        name="packed_rows",
    )(*place, *outs)


def rows_kernel(me_ref, place0, place1, *refs):
    *g_refs, wk_ref, wv_ref, out_ref, grads = refs

    @pl.when(pl.program_id(0) == 0)
    def _():
        half = grads.shape[1] // 2
        for i in range(4):
            part = dot(place0[...], g_refs[2 * i][...], ROWS_LAST)
            part = (part + dot(place1[...], g_refs[2 * i + 1][...], ROWS_LAST)).astype(BF16)
            at = pl.multiple_of((me_ref[0] ^ i) * HEAD_DIM, HEAD_DIM)
            grads[:, pl.ds(at, HEAD_DIM)] = part[:, :HEAD_DIM]
            grads[:, pl.ds(at + half, HEAD_DIM)] = part[:, HEAD_DIM:]

    half = grads.shape[1] // 2
    total = dot(grads[:, :half], wk_ref[...], COLS_LAST)
    out_ref[...] = (total + dot(grads[:, half:], wv_ref[...], COLS_LAST)).astype(BF16)


def row_grads(me, place, parts, w_key, w_value):
    feats, cols = w_key.shape
    rows = place[0].shape[1]
    step = 512
    spec = pltpu.PrefetchScalarGridSpec(
        num_scalar_prefetch=1,
        grid=(feats // step,),
        in_specs=[whole((rows // 2, rows))] * 2
        + [whole((rows // 2, 2 * HEAD_DIM))] * 8
        + [pl.BlockSpec((step, cols), lambda i, me: (i, 0))] * 2,
        out_specs=pl.BlockSpec((rows, step), lambda i, me: (0, i)),
        scratch_shapes=[pltpu.VMEM((rows, 2 * cols), BF16)],
    )
    return pl.pallas_call(
        rows_kernel,
        out_shape=jax.ShapeDtypeStruct((rows, feats), BF16),
        grid_spec=spec,
        compiler_params=params(26),
        cost_estimate=cost(4 * rows * feats * cols, 8 << 20),
        name="row_grads",
    )(me, *place, *parts, w_key, w_value)


def weights_kernel(x_refs, g_refs, out_refs):
    rows = x_refs[0].shape[1]
    group = len(x_refs) // 2
    block = rows // (2 * group)
    grads = []
    for f in range(group):
        g = [(g_refs[2 * (f ^ j) + b], j * block) for b in range(2) for j in range(group)]
        grads.append(jnp.concatenate([ref[at : at + block, :] for ref, at in g], axis=0))
    for side, out_ref in enumerate(out_refs):
        total = None
        for f, g in enumerate(grads):
            term = dot(x_refs[side * group + f][0], g, ROWS_LAST)
            total = term if total is None else total + term
        out_ref[...] = total.astype(out_ref.dtype)


def weight_grads(xs, pieces, half, dtype):
    _, rows, part = xs[0].shape
    out = (part, 2 * HEAD_DIM)

    def kernel(*refs):
        weights_kernel(refs[: len(xs)], refs[len(xs) : -2], refs[-2:])

    return pl.pallas_call(
        kernel,
        out_shape=(jax.ShapeDtypeStruct(out, dtype),) * 2,
        grid=(1,),
        in_specs=[pl.BlockSpec((1, rows, part), lambda i: (half, 0, 0))] * len(xs)
        + [whole(g.shape) for g in pieces],
        out_specs=(whole(out),) * 2,
        compiler_params=params(20),
        cost_estimate=cost(4 * len(xs) * rows * part * HEAD_DIM, 6 << 20),
        name="weight_grads",
    )(*xs, *pieces)


def finish_kernel(learners, me_ref, *refs):
    *sums, k_ref, v_ref = refs
    for i in range(4):
        at = pl.ds(pl.multiple_of((me_ref[0] ^ i) * HEAD_DIM, HEAD_DIM), HEAD_DIM)
        total = (sums[2 * i][...] + sums[2 * i + 1][...].astype(F32)) / learners
        k_ref[:, at] = total[:, :HEAD_DIM]
        v_ref[:, at] = total[:, HEAD_DIM:]


def finish(me, sums, learners):
    part, cols = sums[0].shape
    out = (part, 2 * cols)
    spec = pltpu.PrefetchScalarGridSpec(
        num_scalar_prefetch=1,
        grid=(1,),
        in_specs=[whole((part, cols))] * 8,
        out_specs=(whole(out),) * 2,
    )
    return pl.pallas_call(
        functools.partial(finish_kernel, float(learners)),
        out_shape=(jax.ShapeDtypeStruct(out, F32),) * 2,
        grid_spec=spec,
        compiler_params=params(12),
        cost_estimate=cost(part * cols, 2 << 20),
        name="finish",
    )(me, *sums)


def swap(x, axis, code):
    size = lax.axis_size(axis)
    return lax.ppermute(x, axis, [(i, i ^ code) for i in range(size)])


def after(x, *earlier):
    return lax.optimization_barrier((x,) + earlier)[0]


def local(roll_x, lengths, dest, offsets, queries, out_grad, w_key, w_value):
    learners, heads = lax.axis_size("dp"), lax.axis_size("mp")
    samp, lmax, feats = roll_x.shape
    per = (samp + learners - 1) // learners
    x = roll_x.reshape(samp * lmax, feats)
    m = lax.axis_index("mp").astype(I32).reshape(1)
    d = lax.axis_index("dp").astype(I32).reshape(1)

    away, keep = project(m, x, w_key, w_value, 1)
    core = swap(away, "mp", 1)
    *xs, pick, meta = slots(d, dest, lengths, offsets, after(x, away), learners, per)
    half = after(keep, pick) + core
    across = swap(half, "mp", 2)
    xs_core = [swap(after(xs[0], half), "mp", 1)]
    xs[1:3] = [swap(after(xs[f], half), "dp", f) for f in (1, 2)]
    xs[3] = swap(after(xs[3], xs[1], xs[2]), "dp", 3)
    away, keep = project(m, after(x, xs_core[0]), w_key, w_value, 0)
    core = swap(away, "mp", 1)
    kv = pack(d, keep, core, across, pick, meta)
    kv = lax.all_to_all(kv[0], "dp", split_axis=0, concat_axis=0, tiled=True)
    kv = after(kv, xs[3])

    beyond, out1, place1 = attention(d, kv, queries, out_grad, lmax, learners, 1)
    there = swap(beyond, "dp", 4)
    grads, out0, place0 = attention(d, after(kv, beyond), queries, out_grad, lmax, learners, 0)
    place = [place0, place1]

    xs = xs + xs_core + [swap(b, "mp", 1) for b in xs[1:]]
    near = {(0, 0, 0): grads, (0, 0, 1): there}
    hops = [
        [
            (0, 0, "dp", 1),
            (0, 0, "dp", 2),
            (0, 0, "mp", 2),
            (2, 0, "dp", 1),
            (1, 0, "mp", 2),
            (0, 1, "dp", 2),
            (2, 1, "dp", 1),
        ],
        [
            (0, 0, "dp", 1),
            (0, 0, "dp", 2),
            (0, 0, "mp", 2),
            (2, 0, "dp", 1),
            (1, 0, "mp", 2),
            (0, 1, "dp", 2),
            (1, 1, "dp", 2),
        ],
    ]
    for part, plan in enumerate((hops[0], hops[1])):
        for code, far, axis, step in plan:
            key = (code ^ step, far, part) if axis == "dp" else (code, 1 - far, part)
            near[key] = swap(near[code, far, part], axis, step)
    across = swap(beyond, "mp", 2)
    own = [grads, beyond, swap(grads, "mp", 1), swap(beyond, "mp", 1)]
    own += [near[0, 1, 0], across, swap(near[0, 1, 0], "mp", 1), swap(across, "mp", 1)]
    sums = [None] * 8
    for far in range(2):
        pieces = [near[c, far, b] for c in range(learners // 2) for b in range(2)]
        send = weight_grads(xs, pieces, 1, BF16)
        sums[4 * far + 1] = swap(send[0], "dp", 4)
        sums[4 * far + 3] = swap(send[1], ("dp", "mp"), 4 * heads + 1)
        sums[4 * far], keep = weight_grads(xs, pieces, 0, F32)
        sums[4 * far + 2] = swap(keep, "mp", 1)
    attn_out = packed_rows(place, [out0, out1])
    grad_x = row_grads(m, place, own, w_key, w_value)
    grad_wk, grad_wv = finish(m, sums, learners)
    return (attn_out, grad_x, grad_wk, grad_wv)


def solution(mesh):
    dp, mp = mesh.shape["dp"], mesh.shape["mp"]
    body = local if dp == 8 and mp == 4 else general
    return jax.shard_map(
        body,
        mesh=mesh,
        in_specs=(
            P("dp", None, "mp"),
            P("dp"),
            P("dp"),
            P("dp"),
            P("dp", "mp"),
            P("dp", "mp"),
            P("mp", None),
            P("mp", None),
        ),
        out_specs=(P("dp", "mp"), P("dp", "mp"), P(("mp", "dp"), None), P(("mp", "dp"), None)),
        check_vma=False,
    )
```
